256 devices in a mesh: gx: 64 (over z, y, core), gy: 4 (over x).
Axes of the slice: x: 4, y: 4, z: 8, core: 2. Of those that a mesh axis runs over, the one named last changes fastest.
Arguments:
- velocity_u: float32 [16, 4096, 512], P(None, 'gx', 'gy'), may hold values from -6 to 6
- velocity_v: float32 [16, 4096, 512], P(None, 'gx', 'gy'), may hold values from -6 to 6
- velocity_w: float32 [16, 4096, 512], P(None, 'gx', 'gy'), may hold values from -6 to 6
- potential: float32 [16, 4096, 512], P(None, 'gx', 'gy'), may hold values from -6 to 6
Outputs:
- lorentz: float32 [3, 16, 4096, 512], P(None, None, 'gx', 'gy')
- vorticity: float32 [3, 16, 4096, 512], P(None, None, 'gx', 'gy')
- divergence: float32 [16, 4096, 512], P(None, 'gx', 'gy')
The draws below stay inside these ranges and needn't reach their ends.
All inputs are finite; a program needn't handle non-finite values.
Results may differ from the reference program's by a relative error of at most 0.00005.
Values sent between devices are 32-bit elements; how exact they have to be, the bound alone decides.
No kernel may reach another device: no remote copies, remote signals or barrier semaphores. Data moves between devices by JAX's collectives and lax.ppermute only.
A program may use at most 128 MiB of HBM per device.

```python
import jax
import jax.numpy as jnp
from jax import lax

NZ = 16
NX = 4096
NY = 512


def block_levels(stream_key, shape, pieces, low, top_value):
    loudness = 1.0
    for dim, shards_of in pieces:
        heights = jax.random.uniform(jax.random.fold_in(jax.random.fold_in(stream_key, 6), dim), (shards_of,), jnp.float32, low / len(pieces), top_value / len(pieces))
        loudness = loudness * jnp.repeat(jnp.exp(heights), shape[dim] // shards_of).reshape((-1,) + (1,) * (len(shape) - 1 - dim))
    return loudness


def centred(own_key, extent, width, most, split=(), kind=jnp.bfloat16):
    drawn = width * jax.random.normal(own_key, extent, jnp.float32)
    if split:
        drawn = drawn * block_levels(own_key, extent, split, -0.22, 0.18)
    return jnp.clip(drawn, -most, most).astype(kind)


def setup_inputs(seed: int = 0) -> dict:
    key_of = jax.random.split(jax.random.key(seed), 5)
    return {
        "velocity_u": centred(key_of[0], (NZ, NX, NY), 1.0, 6.0, ((1, 64), (2, 4)), jnp.float32),
        "velocity_v": centred(key_of[1], (NZ, NX, NY), 1.0, 6.0, ((1, 64), (2, 4)), jnp.float32),
        "velocity_w": centred(key_of[2], (NZ, NX, NY), 1.0, 6.0, ((1, 64), (2, 4)), jnp.float32),
        "potential": centred(key_of[3], (NZ, NX, NY), 1.0, 6.0, ((1, 64), (2, 4)), jnp.float32),
    }


alpha_inner = 1.0 / 3.0
coef_near = 7.0 / 9.0
coef_far = 1.0 / 36.0
field_bx = 0.6
field_by = 0.8

def z_derivative(field, axis):

    def plus(k):
        return jnp.roll(field, -k, axis) - jnp.roll(field, k, axis)
    return 0.75 * plus(1) - 0.15 * plus(2) + plus(3) / 60.0

def wall_coefficients(rows, total):
    edge = (rows == 1) | (rows == total - 2)
    lower = jnp.where(rows == 0, 0.0, jnp.where(edge, 0.25, jnp.where(rows == total - 1, 2.0, alpha_inner)))
    upper = jnp.where(rows == total - 1, 0.0, jnp.where(edge, 0.25, jnp.where(rows == 0, 2.0, alpha_inner)))
    return (lower.astype(jnp.float32), upper.astype(jnp.float32))

def x_derivative(field):
    count = field.shape[1]
    spectrum = jnp.fft.rfft(field, axis=1)
    theta = 2.0 * jnp.pi * jnp.arange(count // 2 + 1).astype(field.dtype) / count
    symbol = (2.0 * coef_near * jnp.sin(theta) + 2.0 * coef_far * jnp.sin(2.0 * theta)) / (1.0 + 2.0 * alpha_inner * jnp.cos(theta))
    result = jnp.fft.irfft(spectrum * (1j * symbol)[None, :, None], n=count, axis=1)
    return result.astype(field.dtype)

def y_derivative(field):
    total = field.shape[2]
    padded = jnp.pad(field, ((0, 0), (0, 0), (2, 2)))
    right = coef_near * (padded[:, :, 3:-1] - padded[:, :, 1:-3]) + coef_far * (padded[:, :, 4:] - padded[:, :, :-4])
    right = right.at[:, :, 0].set(-2.5 * field[:, :, 0] + 2.0 * field[:, :, 1] + 0.5 * field[:, :, 2])
    right = right.at[:, :, 1].set(0.75 * (field[:, :, 2] - field[:, :, 0]))
    right = right.at[:, :, total - 2].set(0.75 * (field[:, :, total - 1] - field[:, :, total - 3]))
    right = right.at[:, :, total - 1].set(2.5 * field[:, :, total - 1] - 2.0 * field[:, :, total - 2] - 0.5 * field[:, :, total - 3])
    lower, upper = wall_coefficients(jnp.arange(total, dtype=jnp.int32), total)
    diagonal = jnp.ones((total,), field.dtype)
    columns = right.reshape(-1, total).T
    solved = lax.linalg.tridiagonal_solve(lower.astype(field.dtype), diagonal, upper.astype(field.dtype), columns)
    return solved.T.reshape(field.shape)

def assemble(stacked, x_deriv, y_deriv, z_deriv):
    current_x = -x_deriv[3] - field_by * stacked[2]
    current_y = -y_deriv[3] + field_bx * stacked[2]
    current_z = -z_deriv[3] + field_by * stacked[0] - field_bx * stacked[1]
    lorentz = jnp.stack([-field_by * current_z, field_bx * current_z, field_by * current_x - field_bx * current_y])
    vorticity = jnp.stack([y_deriv[2] - z_deriv[1], z_deriv[0] - x_deriv[2], x_deriv[1] - y_deriv[0]])
    divergence = x_deriv[0] + y_deriv[1] + z_deriv[2]
    return (lorentz, vorticity, divergence)

def reference(velocity_u, velocity_v, velocity_w, potential):
    fields = [velocity_u, velocity_v, velocity_w, potential]
    stacked = jnp.stack(fields)
    x_deriv = jnp.stack([x_derivative(f) for f in fields])
    y_deriv = jnp.stack([y_derivative(f) for f in fields])
    z_deriv = z_derivative(stacked, 1)
    lorentz, vorticity, divergence = assemble(stacked, x_deriv, y_deriv, z_deriv)
    return (lorentz, vorticity, divergence)
```

```python
import functools
import math

import jax
import jax.numpy as jnp
import ml_dtypes
import numpy as np
from jax import lax
from jax.experimental import pallas as pl
from jax.experimental.pallas import tpu as pltpu
from jax.sharding import PartitionSpec as P

third = 1.0 / 3.0
near = 7.0 / 9.0
far = 1.0 / 36.0
bx = 0.6
by = 0.8

lam = (-3.0 + math.sqrt(5.0)) / 2.0
scale = 1.0 / (1.0 + 2.0 * third * lam)
log_lam = math.log(-lam)
gamma = scale * (near * (lam - 1.0 / lam) + far * (lam**2 - lam**-2))
edge = scale * (near * (lam**2 - 1.0) + far * (lam**3 - lam)) - gamma * lam

f32 = jnp.float32
bf16 = jnp.bfloat16


def halves(values):
    high = values.astype(bf16)
    return high, (values - high.astype(f32)).astype(bf16)


def host_halves(values):
    values = values.astype(np.float32)
    high = values.astype(ml_dtypes.bfloat16)
    low = (values - high.astype(np.float32)).astype(ml_dtypes.bfloat16)
    return high, low


def x_operator(count):
    h = lambda m: scale * lam ** np.abs(m)
    i = np.arange(count)
    m = i[:, None] - i[None, :]
    own = near * (h(m + 1) - h(m - 1)) + far * (h(m + 2) - h(m - 2))
    high, low = host_halves(own)
    return np.concatenate([high, low, high], axis=1)


def y_operators(total, blocks):
    a = np.eye(total)
    b = np.zeros((total, total))
    for j in range(2, total - 2):
        a[j, j - 1] = a[j, j + 1] = third
        b[j, j + 1], b[j, j - 1], b[j, j + 2], b[j, j - 2] = near, -near, far, -far
    a[0, 1] = a[-1, -2] = 2.0
    b[0, :3] = -2.5, 2.0, 0.5
    b[-1, -3:] = -0.5, -2.0, 2.5
    for j in (1, total - 2):
        a[j, j - 1] = a[j, j + 1] = 0.25
        b[j, j + 1], b[j, j - 1] = 0.75, -0.75
    whole = np.linalg.solve(a, b)
    size = total // blocks
    out = []
    for g in range(blocks):
        own = whole[g * size : (g + 1) * size, g * size : (g + 1) * size].T
        high, low = host_halves(own)
        out.append(np.block([[high, low], [high, np.zeros_like(low)]]))
    return np.stack(out)


def power(n):
    size = jnp.exp(n.astype(f32) * log_lam)
    return jnp.where((n & 1) == 0, size, -size)


def edges_kernel(u, v, w, p, fields, msg_a, msg_b, msg_c, msg_d, sems):
    sources = (u, v, w, p)
    copies = [pltpu.make_async_copy(s, fields.at[i], sems.at[i]) for i, s in enumerate(sources)]
    for c in copies:
        c.start()
    depth, rows, lanes = u.shape
    even_x = lax.rem(lax.axis_index("gx"), 2) == 0
    even_y = lax.rem(lax.axis_index("gy"), 2) == 0

    k = lax.broadcasted_iota(jnp.int32, (rows, lanes), 0)
    to_right = gamma * power(rows - k)
    to_left = -gamma * power(k + 1)
    weights_a = jnp.where(even_x, to_right, to_left)
    weights_b = jnp.where(even_x, to_left, to_right)

    j = lax.broadcasted_iota(jnp.int32, (8, lanes), 1)
    row = lax.broadcasted_iota(jnp.int32, (8, lanes), 0)
    y_right = jnp.where((row & 1) == 0, gamma * power(lanes - j), jnp.where(j == lanes - 1, edge, 0.0))
    y_left = jnp.where((row & 1) == 0, -gamma * power(j + 1), jnp.where(j == 0, -edge, 0.0))
    rightward = (row < 2) == even_y
    high, low = halves(jnp.where(rightward, y_right, y_left))
    both = jnp.concatenate([high, low], axis=0)

    for i in range(4):
        copies[i].wait()
        f = fields[i]
        first, last = f[:, 0, :], f[:, rows - 1, :]
        rr, ll = edge * last, -edge * first
        msg_a[pl.ds(2 * i * depth, depth), :] = jnp.sum(f * weights_a[None], axis=1)
        msg_a[pl.ds((2 * i + 1) * depth, depth), :] = jnp.where(even_x, rr, ll)
        msg_b[pl.ds(2 * i * depth, depth), :] = jnp.sum(f * weights_b[None], axis=1)
        msg_b[pl.ds((2 * i + 1) * depth, depth), :] = jnp.where(even_x, ll, rr)
    nt = (((1,), (1,)), ((), ()))
    for i in range(4):
        fh, fl = halves(fields[i].reshape(depth * rows, lanes))
        top = lax.dot_general(both, fh, nt, preferred_element_type=f32)
        rest = lax.dot_general(both, fl, nt, preferred_element_type=f32)
        sums = top[0:8] + top[8:16] + rest[0:8]
        msg_c[pl.ds(2 * i, 2), :] = sums[0:2]
        msg_d[pl.ds(2 * i, 2), :] = sums[2:4]


def local_kernel(fields, wx, wy_all, lorentz, lz_o, vx_o, vy_o, vz_o, dv_o, wy, lx_s, ly_s, sems):
    gy = lax.axis_index("gy")
    get = pltpu.make_async_copy(wy_all.at[gy], wy, sems.at[0])
    get.start()
    _, depth, rows, lanes = fields.shape
    u, v, w, p = range(4)

    def dz(i, k):
        at = lambda s: fields[i, (k + s) % depth]
        return (
            0.75 * (at(1) - at(-1)) - 0.15 * (at(2) - at(-2)) + (1.0 / 60.0) * (at(3) - at(-3))
        )

    for k in range(depth):
        jz = by * fields[u, k] - bx * fields[v, k] - dz(p, k)
        lx_s[k] = -by * jz
        ly_s[k] = bx * jz
    put_x = pltpu.make_async_copy(lx_s, lorentz.at[0], sems.at[1])
    put_y = pltpu.make_async_copy(ly_s, lorentz.at[1], sems.at[2])
    put_x.start()
    put_y.start()
    get.wait()
    for k in range(depth):
        split = [halves(fields[i, k]) for i in range(4)]
        highs = jnp.concatenate([s[0] for s in split], axis=0)
        lows = jnp.concatenate([s[1] for s in split], axis=0)
        y = jnp.dot(
            jnp.concatenate([highs, lows], axis=1), wy[...], preferred_element_type=f32
        )
        y = y[:, :lanes] + y[:, lanes:]
        wide_h = jnp.concatenate([s[0] for s in split], axis=1)
        wide_l = jnp.concatenate([s[1] for s in split], axis=1)
        x = jnp.dot(
            wx[...], jnp.concatenate([wide_h, wide_h, wide_l], axis=0), preferred_element_type=f32
        )
        yd = lambda i: y[i * rows : (i + 1) * rows]
        xd = lambda i: x[:, i * lanes : (i + 1) * lanes]
        lz_o[k] = bx * yd(p) - by * xd(p) - fields[w, k]
        vx_o[k] = yd(w) - dz(v, k)
        vy_o[k] = dz(u, k) - xd(w)
        vz_o[k] = xd(v) - yd(u)
        dv_o[k] = xd(u) + yd(v) + dz(w, k)
    put_x.wait()
    put_y.wait()


def join_kernel(
    got_a, got_b, got_c, got_d, lz, vx, vy, vz, dv, lorentz_in, lorentz, vorticity, divergence,
    lz_s, vx_s, vy_s, vz_s, dv_s, sems
):
    depth, rows, lanes = lz.shape
    gy, blocks = lax.axis_index("gy"), lax.axis_size("gy")
    even_x = lax.rem(lax.axis_index("gx"), 2) == 0
    even_y = lax.rem(gy, 2) == 0
    inner = jnp.logical_and(gy > 0, gy < blocks - 1)

    width = 4 * lanes
    lane = lax.broadcasted_iota(jnp.int32, (16, width), 1)
    row = lax.broadcasted_iota(jnp.int32, (16, width), 0)
    j = lane & (lanes - 1)
    left = jnp.where((row & 1) == 0, power(j), jnp.where(j == 0, 1.0, 0.0))
    right = jnp.where((row & 1) == 0, power(lanes - 1 - j), jnp.where(j == lanes - 1, 1.0, 0.0))
    from_d = row >= 8
    spread = jnp.where(from_d == even_y, left, right)
    field = (row & 7) >> 1
    target = lane // lanes
    hit = jnp.where(field == 0, 2, jnp.where(field == 1, 3, jnp.where(field == 2, 1, 0))) == target
    factor = jnp.where(target == 0, bx, jnp.where(target == 2, -1.0, 1.0))
    spread = jnp.where(hit, spread * factor, 0.0)
    spread = jnp.where(jnp.logical_and(from_d, jnp.logical_not(inner)), 0.0, spread)
    sh, sl = halves(spread)
    spread3 = jnp.concatenate([sh, sh, sl], axis=0)
    mh, ml = halves(jnp.concatenate([got_c[...], got_d[...]], axis=0))
    sums3 = jnp.concatenate([mh, ml, mh], axis=0)

    i = lax.broadcasted_iota(jnp.int32, (rows, lanes), 0)
    fall_l, fall_r = power(i), power(rows - 1 - i)
    hit_l, hit_r = jnp.where(i == 0, 1.0, 0.0), jnp.where(i == rows - 1, 1.0, 0.0)
    ta, ea = jnp.where(even_x, fall_r, fall_l), jnp.where(even_x, hit_r, hit_l)
    tb, eb = jnp.where(even_x, fall_l, fall_r), jnp.where(even_x, hit_l, hit_r)

    def xc(f, k):
        at = lambda ref, kind: ref[pl.ds((2 * f + kind) * depth + k, 1), :]
        return ta * at(got_a, 0) + ea * at(got_a, 1) + tb * at(got_b, 0) + eb * at(got_b, 1)

    group = 2
    tn = (((0,), (0,)), ((), ()))
    for g in range(depth // group):
        span = group * rows
        yc = lax.dot_general(
            sums3[:, g * span : (g + 1) * span], spread3, tn, preferred_element_type=f32
        )
        for q in range(group):
            k = g * group + q
            part = lambda t: yc[q * rows : (q + 1) * rows, t * lanes : (t + 1) * lanes]
            lz_s[k] = lz[k] + part(0) - by * xc(3, k)
            vx_s[k] = vx[k] + part(1)
            vy_s[k] = vy[k] - xc(2, k)
            vz_s[k] = vz[k] + part(2) + xc(1, k)
            dv_s[k] = dv[k] + part(3) + xc(0, k)
    copies = [
        pltpu.make_async_copy(s, d, sems.at[n])
        for n, (s, d) in enumerate(
            [
                (lz_s, lorentz.at[2]),
                (vx_s, vorticity.at[0]),
                (vy_s, vorticity.at[1]),
                (vz_s, vorticity.at[2]),
                (dv_s, divergence),
            ]
        )
    ]
    for c in copies:
        c.start()
    for c in copies:
        c.wait()


def local(wx, wy, ring, line, u, v, w, p):
    depth, rows, lanes = u.shape
    block = (depth, rows, lanes)
    vmem = pl.BlockSpec(memory_space=pltpu.VMEM)
    anywhere = pl.BlockSpec(memory_space=pl.ANY)
    params = pltpu.CompilerParams(vmem_limit_bytes=24 * 2**20)
    keep = lambda x: pltpu.with_memory_space_constraint(x, pltpu.VMEM)
    size = 4 * depth * rows * lanes

    fields, msg_a, msg_b, msg_c, msg_d = pl.pallas_call(
        edges_kernel,
        name="edge_sums",
        out_shape=(
            pltpu.VMEM((4,) + block, f32),
            pltpu.VMEM((8 * depth, lanes), f32),
            pltpu.VMEM((8 * depth, lanes), f32),
            pltpu.VMEM((8, depth * rows), f32),
            pltpu.VMEM((8, depth * rows), f32),
        ),
        in_specs=[anywhere] * 4,
        out_specs=(vmem,) * 5,
        scratch_shapes=[pltpu.SemaphoreType.DMA((4,))],
        compiler_params=params,
        cost_estimate=pl.CostEstimate(flops=8 * size, bytes_accessed=4 * size, transcendentals=0),
    )(u, v, w, p)

    pairs_a = [(i, i ^ 1) for i in range(ring)]
    pairs_b = [(i, (i + 1) % ring if i % 2 else (i - 1) % ring) for i in range(ring)]
    pairs_c = [(i, i ^ 1) for i in range(line)]
    pairs_d = [(i, (i + 1) % line if i % 2 else (i - 1) % line) for i in range(line)]
    got_b = lax.ppermute(msg_b, "gx", pairs_b)
    got_a = lax.ppermute(msg_a, "gx", pairs_a)
    got_c = lax.ppermute(msg_c, "gy", pairs_c)
    got_d = lax.ppermute(msg_d, "gy", pairs_d)

    lorentz, lz, vx, vy, vz, dv = pl.pallas_call(
        local_kernel,
        name="own_block",
        out_shape=(jax.ShapeDtypeStruct((3,) + block, f32),) + (pltpu.VMEM(block, f32),) * 5,
        in_specs=[vmem, vmem, anywhere],
        out_specs=(anywhere,) + (vmem,) * 5,
        scratch_shapes=[
            pltpu.VMEM((2 * lanes, 2 * lanes), bf16),
            pltpu.VMEM(block, f32),
            pltpu.VMEM(block, f32),
            pltpu.SemaphoreType.DMA((3,)),
        ],
        compiler_params=params,
        cost_estimate=pl.CostEstimate(flops=800 * size, bytes_accessed=12 * size, transcendentals=0),
    )(keep(fields), jnp.asarray(wx), jnp.asarray(wy))

    return pl.pallas_call(
        join_kernel,
        name="join",
        out_shape=(
            jax.ShapeDtypeStruct((3,) + block, f32),
            jax.ShapeDtypeStruct((3,) + block, f32),
            jax.ShapeDtypeStruct(block, f32),
        ),
        in_specs=[vmem] * 9 + [anywhere],
        out_specs=(anywhere,) * 3,
        scratch_shapes=[pltpu.VMEM(block, f32)] * 5 + [pltpu.SemaphoreType.DMA((5,))],
        input_output_aliases={9: 0},
        compiler_params=params,
        cost_estimate=pl.CostEstimate(flops=30 * size, bytes_accessed=12 * size, transcendentals=0),
    )(
        *(keep(x) for x in (got_a, got_b, got_c, got_d, lz, vx, vy, vz, dv)),
        lorentz,
    )


def solution(mesh):
    ring, line = mesh.shape["gx"], mesh.shape["gy"]
    cells = P(None, "gx", "gy")
    stacked = P(None, None, "gx", "gy")
    wx = x_operator(4096 // ring)
    wy = y_operators(512, line)
    return jax.shard_map(
        functools.partial(local, wx, wy, ring, line),
        mesh=mesh,
        in_specs=(cells,) * 4,
        out_specs=(stacked, stacked, cells),
        check_vma=False,
    )
```

```python
import functools
import math

import jax
import jax.numpy as jnp
import ml_dtypes
import numpy as np
from jax import lax
from jax.experimental import pallas as pl
from jax.experimental.pallas import tpu as pltpu
from jax.sharding import PartitionSpec as P

third = 1.0 / 3.0
near = 7.0 / 9.0
far = 1.0 / 36.0
bx = 0.6
by = 0.8

lam = (-3.0 + math.sqrt(5.0)) / 2.0
scale = 1.0 / (1.0 + 2.0 * third * lam)
log_lam = math.log(-lam)
gamma = scale * (near * (lam - 1.0 / lam) + far * (lam**2 - lam**-2))
edge = scale * (near * (lam**2 - 1.0) + far * (lam**3 - lam)) - gamma * lam

f32 = jnp.float32
bf16 = jnp.bfloat16
pieces = 2


def halves(values):
    high = values.astype(bf16)
    return high, (values - high.astype(f32)).astype(bf16)


def host_halves(values):
    values = values.astype(np.float32)
    high = values.astype(ml_dtypes.bfloat16)
    low = (values - high.astype(np.float32)).astype(ml_dtypes.bfloat16)
    return high, low


def x_operator(count):
    h = lambda m: scale * lam ** np.abs(m)
    i = np.arange(count)
    m = i[:, None] - i[None, :]
    own = near * (h(m + 1) - h(m - 1)) + far * (h(m + 2) - h(m - 2))
    high, low = host_halves(own)
    return np.concatenate([high, low, high], axis=1)


def y_operators(total, blocks):
    a = np.eye(total)
    b = np.zeros((total, total))
    for j in range(2, total - 2):
        a[j, j - 1] = a[j, j + 1] = third
        b[j, j + 1], b[j, j - 1], b[j, j + 2], b[j, j - 2] = near, -near, far, -far
    a[0, 1] = a[-1, -2] = 2.0
    b[0, :3] = -2.5, 2.0, 0.5
    b[-1, -3:] = -0.5, -2.0, 2.5
    for j in (1, total - 2):
        a[j, j - 1] = a[j, j + 1] = 0.25
        b[j, j + 1], b[j, j - 1] = 0.75, -0.75
    whole = np.linalg.solve(a, b)
    size = total // blocks
    out = []
    for g in range(blocks):
        own = whole[g * size : (g + 1) * size, g * size : (g + 1) * size].T
        high, low = host_halves(own)
        out.append(np.block([[high, low], [high, np.zeros_like(low)]]))
    return np.stack(out)


def power(n):
    size = jnp.exp(n.astype(f32) * log_lam)
    return jnp.where((n & 1) == 0, size, -size)


def x_message(f, msg, planes, at_right):
    depth, rows, lanes = f.shape
    k = lax.broadcasted_iota(jnp.int32, (rows, lanes), 0)
    weights = jnp.where(at_right, gamma * power(rows - k), -gamma * power(k + 1))
    msg[0, planes] = jnp.sum(f * weights[None], axis=1)
    msg[1, planes] = jnp.where(at_right, edge * f[:, rows - 1, :], -edge * f[:, 0, :])


def y_messages(fields, msg_c, msg_d):
    _, depth, rows, lanes = fields.shape
    even_y = lax.rem(lax.axis_index("gy"), 2) == 0
    j = lax.broadcasted_iota(jnp.int32, (8, lanes), 1)
    row = lax.broadcasted_iota(jnp.int32, (8, lanes), 0)
    odd = (row & 1) == 1
    y_right = jnp.where(odd, jnp.where(j == lanes - 1, edge, 0.0), gamma * power(lanes - j))
    y_left = jnp.where(odd, jnp.where(j == 0, -edge, 0.0), -gamma * power(j + 1))
    high, low = halves(jnp.where((row < 2) == even_y, y_right, y_left))
    both = jnp.concatenate([high, low], axis=0)
    nt = (((1,), (1,)), ((), ()))
    for i in range(4):
        fh, fl = halves(fields[i].reshape(depth * rows, lanes))
        top = lax.dot_general(both, fh, nt, preferred_element_type=f32)
        rest = lax.dot_general(both, fl, nt, preferred_element_type=f32)
        sums = top[0:8] + top[8:16] + rest[0:8]
        for b in range(depth * rows // lanes):
            part = sums[:, b * lanes : (b + 1) * lanes]
            msg_c[pl.ds(8 * b + 2 * i, 2), :] = part[0:2]
            msg_d[pl.ds(8 * b + 2 * i, 2), :] = part[2:4]


def edges_kernel(u, v, w, p, fields, chip, far_side, early_c, early_d, sems):
    depth, rows, lanes = u.shape
    piece = depth // pieces
    copies = [
        [
            pltpu.make_async_copy(
                s.at[pl.ds(n * piece, piece)],
                fields.at[i, pl.ds(n * piece, piece)],
                sems.at[i * pieces + n],
            )
            for n in range(pieces)
        ]
        for i, s in enumerate((u, v, w, p))
    ]
    for field in copies:
        for c in field:
            c.start()
    gx = lax.axis_index("gx")
    even_x = lax.rem(gx, 2) == 0
    early_d[...] = jnp.zeros_like(early_d)
    for i in range(4):
        for n in range(pieces):
            copies[i][n].wait()
            f = fields[i, pl.ds(n * piece, piece)]
            planes = pl.ds(n * piece, piece)
            x_message(f, chip.at[i], planes, even_x)
            x_message(f, far_side.at[i], planes, jnp.logical_not(even_x))

    @pl.when(gx < 2)
    def _():
        early_c[...] = jnp.zeros_like(early_c)
        y_messages(fields, early_c, early_d)

    @pl.when(gx >= 2)
    def _():
        early_c[...] = chip[...].reshape(early_c.shape)


def late_kernel(fields, chip, early_c, early_d, late_c, late_d):
    @pl.when(lax.axis_index("gx") < 2)
    def _():
        late_c[...] = chip[...].reshape(late_c.shape)
        late_d[...] = jnp.zeros_like(late_d)

    @pl.when(lax.axis_index("gx") >= 2)
    def _():
        y_messages(fields, late_c, late_d)


def own_kernel(fields, wx, wy_all, lorentz, lz_o, vx_o, vy_o, vz_o, dv_o, lx_s, ly_s, sems):
    _, depth, rows, lanes = fields.shape
    u, v, w, p = range(4)
    wy = wy_all.at[lax.axis_index("gy")]

    def dz(i, k):
        at = lambda s: fields[i, (k + s) % depth]
        return (
            0.75 * (at(1) - at(-1)) - 0.15 * (at(2) - at(-2)) + (1.0 / 60.0) * (at(3) - at(-3))
        )

    for k in range(depth):
        jz = by * fields[u, k] - bx * fields[v, k] - dz(p, k)
        lx_s[k] = -by * jz
        ly_s[k] = bx * jz
    put_x = pltpu.make_async_copy(lx_s, lorentz.at[0], sems.at[0])
    put_y = pltpu.make_async_copy(ly_s, lorentz.at[1], sems.at[1])
    put_x.start()
    put_y.start()
    for k in range(depth):
        split = [halves(fields[i, k]) for i in range(4)]
        highs = jnp.concatenate([s[0] for s in split], axis=0)
        lows = jnp.concatenate([s[1] for s in split], axis=0)
        y = jnp.dot(jnp.concatenate([highs, lows], axis=1), wy[...], preferred_element_type=f32)
        y = y[:, :lanes] + y[:, lanes:]
        wide_h = jnp.concatenate([s[0] for s in split], axis=1)
        wide_l = jnp.concatenate([s[1] for s in split], axis=1)
        x = jnp.dot(
            wx[...], jnp.concatenate([wide_h, wide_h, wide_l], axis=0), preferred_element_type=f32
        )
        yd = lambda i: y[i * rows : (i + 1) * rows]
        xd = lambda i: x[:, i * lanes : (i + 1) * lanes]
        lz_o[k] = bx * yd(p) - by * xd(p) - fields[w, k]
        vx_o[k] = yd(w) - dz(v, k)
        vy_o[k] = dz(u, k) - xd(w)
        vz_o[k] = xd(v) - yd(u)
        dv_o[k] = xd(u) + yd(v) + dz(w, k)
    put_x.wait()
    put_y.wait()


def hold_kernel(message, held):
    pass


def y_spread(lanes, line):
    out = []
    j = np.arange(lanes)
    for g in range(line):
        table = np.zeros((16, 4, lanes))
        for side in range(2):
            from_left = (side == 1) == (g % 2 == 0)
            if (from_left and g == 0) or (not from_left and g == line - 1):
                continue
            away = j if from_left else lanes - 1 - j
            for field, (target, factor) in enumerate(((2, -1.0), (3, 1.0), (1, 1.0), (0, bx))):
                table[8 * side + 2 * field, target] = factor * lam**away
                table[8 * side + 2 * field + 1, target] = factor * (away == 0)
        table = table.reshape(16, 4 * lanes)
        table[np.abs(table) < 1e-37] = 0.0
        high, low = host_halves(table)
        out.append(np.concatenate([high, high, low], axis=0))
    return np.stack(out)


def join_kernel(
    got_far, early_c, early_d, late_c, late_d, spread_all, lz, vx, vy, vz, dv, lorentz_in,
    lorentz, vorticity, divergence, lz_s, vx_s, vy_s, vz_s, dv_s, chip_s, sems
):
    depth, rows, lanes = lz.shape
    gx = lax.axis_index("gx")
    even_x = lax.rem(gx, 2) == 0
    first = gx < 2
    spread = spread_all[lax.axis_index("gy")]
    got_c = jnp.where(first, early_c[...], late_c[...])
    got_d = jnp.where(first, early_d[...], late_d[...])
    chip_s[...] = jnp.where(first, late_c[...], early_c[...])
    i = lax.broadcasted_iota(jnp.int32, (rows, lanes), 0)
    fall_l, fall_r = power(i), power(rows - 1 - i)
    fall_chip = jnp.where(even_x, fall_r, fall_l)
    fall_far = jnp.where(even_x, fall_l, fall_r)
    sub = lax.broadcasted_iota(jnp.int32, (8, lanes), 0)
    low_far = jnp.where(jnp.logical_and(sub == 0, even_x), 1.0, 0.0)
    low_chip = jnp.where(jnp.logical_and(sub == 0, jnp.logical_not(even_x)), 1.0, 0.0)
    high_far = jnp.where(jnp.logical_and(sub == 7, jnp.logical_not(even_x)), 1.0, 0.0)
    high_chip = jnp.where(jnp.logical_and(sub == 7, even_x), 1.0, 0.0)

    def xc(f, k):
        at = lambda ref, kind: ref[pl.ds((2 * f + kind) * depth + k, 1), :]
        c = fall_far * at(got_far, 0) + fall_chip * at(chip_s, 0)
        far_e, chip_e = at(got_far, 1), at(chip_s, 1)
        head = c[:8] + low_far * far_e + low_chip * chip_e
        tail = c[rows - 8 :] + high_far * far_e + high_chip * chip_e
        return jnp.concatenate([head, c[8 : rows - 8], tail], axis=0)

    group = 4
    per = lanes // rows
    tn = (((0,), (0,)), ((), ()))
    copies = []
    for g in range(depth // group):
        for k in range(g * group, (g + 1) * group):
            b, q = k // per, k % per
            if q == 0:
                got = [m[8 * b : 8 * b + 8] for m in (got_c, got_d)]
                high, low = halves(jnp.concatenate(got, axis=0))
                sums = jnp.concatenate([high, low, high], axis=0)
                yc = lax.dot_general(sums, spread, tn, preferred_element_type=f32)
            part = lambda t: yc[q * rows : (q + 1) * rows, t * lanes : (t + 1) * lanes]
            lz_s[k] = lz[k] + part(0) - by * xc(3, k)
            vx_s[k] = vx[k] + part(1)
            vy_s[k] = vy[k] - xc(2, k)
            vz_s[k] = vz[k] + part(2) + xc(1, k)
            dv_s[k] = dv[k] + part(3) + xc(0, k)
        planes = pl.ds(g * group, group)
        for s, d in (
            (lz_s, lorentz.at[2]),
            (vx_s, vorticity.at[0]),
            (vy_s, vorticity.at[1]),
            (vz_s, vorticity.at[2]),
            (dv_s, divergence),
        ):
            c = pltpu.make_async_copy(s.at[planes], d.at[planes], sems.at[len(copies)])
            c.start()
            copies.append(c)
    for c in copies:
        c.wait()


def local(wx, wy, spread, ring, line, u, v, w, p):
    depth, rows, lanes = u.shape
    block = (depth, rows, lanes)
    vmem = pl.BlockSpec(memory_space=pltpu.VMEM)
    anywhere = pl.BlockSpec(memory_space=pl.ANY)
    params = pltpu.CompilerParams(vmem_limit_bytes=24 * 2**20)
    keep = lambda x: pltpu.with_memory_space_constraint(x, pltpu.VMEM)
    stay = lambda x: pltpu.with_memory_space_constraint(x, pltpu.HBM)
    size = 4 * depth * rows * lanes
    cost = lambda flops, moved: pl.CostEstimate(
        flops=flops * size, bytes_accessed=moved * size, transcendentals=0
    )
    wx, wy, spread = (keep(jnp.asarray(t)) for t in (wx, wy, spread))
    msg = pltpu.VMEM((8 * depth, lanes), f32)
    x_msg = pltpu.VMEM((4, 2, depth, lanes), f32)
    half = pltpu.VMEM((4 * depth, lanes), f32)

    def over_chips(column):
        return [
            (i * line + j, column(i, j)[0] * line + column(i, j)[1])
            for i in range(ring)
            for j in range(line)
        ]

    mate = lambda i, j: (i ^ 1, j)
    y_one = lambda i, j: (i, j ^ 1)
    y_two = lambda i, j: (i, (j + 1) % line if j % 2 else (j - 1) % line)
    first = lambda a, b: over_chips(lambda i, j: a(i, j) if i < 2 else b(i, j))
    both = ("gx", "gy")

    fields, chip, far_side, early_c, early_d = pl.pallas_call(
        edges_kernel,
        name="edge_sums",
        out_shape=(pltpu.VMEM((4,) + block, f32), x_msg, x_msg, msg, half),
        in_specs=[anywhere] * 4,
        out_specs=(vmem,) * 5,
        scratch_shapes=[pltpu.SemaphoreType.DMA((4 * pieces,))],
        compiler_params=params,
        cost_estimate=cost(1, 1),
    )(*(stay(x) for x in (u, v, w, p)))
    early_c = lax.ppermute(early_c, both, first(y_one, mate))
    early_d = lax.ppermute(early_d, both, first(y_two, mate))

    far_side = pl.pallas_call(
        hold_kernel,
        name="hold",
        out_shape=x_msg,
        in_specs=[vmem],
        out_specs=vmem,
        input_output_aliases={0: 0},
        compiler_params=params,
        cost_estimate=cost(1, 1),
    )(keep(far_side))
    got_far = lax.ppermute(
        far_side, "gx", [(i, (i + 1) % ring if i % 2 else (i - 1) % ring) for i in range(ring)]
    )

    late_c, late_d = pl.pallas_call(
        late_kernel,
        name="y_sums",
        out_shape=(msg, half),
        in_specs=[vmem, vmem, anywhere, anywhere],
        out_specs=(vmem,) * 2,
        compiler_params=params,
        cost_estimate=cost(1, 1),
    )(*(keep(x) for x in (fields, chip, early_c, early_d)))
    late_c = lax.ppermute(late_c, both, first(mate, y_one))
    late_d = lax.ppermute(late_d, both, first(mate, y_two))

    lorentz, *part = pl.pallas_call(
        own_kernel,
        name="own_block",
        out_shape=(jax.ShapeDtypeStruct((3,) + block, f32),) + (pltpu.VMEM(block, f32),) * 5,
        in_specs=[vmem] * 3,
        out_specs=(anywhere,) + (vmem,) * 5,
        scratch_shapes=[
            pltpu.VMEM(block, f32),
            pltpu.VMEM(block, f32),
            pltpu.SemaphoreType.DMA((2,)),
        ],
        compiler_params=params,
        cost_estimate=cost(4000, 12),
    )(keep(fields), wx, wy)

    got_far = got_far.reshape(msg.shape)
    return pl.pallas_call(
        join_kernel,
        name="join",
        out_shape=(
            jax.ShapeDtypeStruct((3,) + block, f32),
            jax.ShapeDtypeStruct((3,) + block, f32),
            jax.ShapeDtypeStruct(block, f32),
        ),
        in_specs=[vmem] * 11 + [anywhere],
        out_specs=(anywhere,) * 3,
        scratch_shapes=[pltpu.VMEM(block, f32)] * 5
        + [pltpu.VMEM(msg.shape, f32), pltpu.SemaphoreType.DMA((20,))],
        input_output_aliases={11: 0},
        compiler_params=params,
        cost_estimate=cost(30, 12),
    )(
        *(keep(x) for x in (got_far, early_c, early_d, late_c, late_d)),
        spread,
        *(keep(x) for x in part),
        lorentz,
    )


def solution(mesh):
    ring, line = mesh.shape["gx"], mesh.shape["gy"]
    cells = P(None, "gx", "gy")
    stacked = P(None, None, "gx", "gy")
    wx = x_operator(4096 // ring)
    wy = y_operators(512, line)
    spread = y_spread(512 // line, line)
    return jax.shard_map(
        functools.partial(local, wx, wy, spread, ring, line),
        mesh=mesh,
        in_specs=(cells,) * 4,
        out_specs=(stacked, stacked, cells),
        check_vma=False,
    )
```

```python
import functools
import math

import jax
import jax.numpy as jnp
import ml_dtypes
import numpy as np
from jax import lax
from jax.experimental import pallas as pl
from jax.experimental.pallas import tpu as pltpu
from jax.sharding import PartitionSpec as P

third = 1.0 / 3.0
near = 7.0 / 9.0
far = 1.0 / 36.0
bx = 0.6
by = 0.8

lam = (-3.0 + math.sqrt(5.0)) / 2.0
scale = 1.0 / (1.0 + 2.0 * third * lam)
log_lam = math.log(-lam)
gamma = scale * (near * (lam - 1.0 / lam) + far * (lam**2 - lam**-2))
edge = scale * (near * (lam**2 - 1.0) + far * (lam**3 - lam)) - gamma * lam

f32 = jnp.float32
bf16 = jnp.bfloat16
pieces = 1
own_step = 8
join_groups = (2, 2, 2, 2, 2, 2, 2, 2)


def halves(values):
    high = values.astype(bf16)
    return high, (values - high.astype(f32)).astype(bf16)


def host_halves(values):
    values = values.astype(np.float32)
    high = values.astype(ml_dtypes.bfloat16)
    low = (values - high.astype(np.float32)).astype(ml_dtypes.bfloat16)
    return high, low


def x_operator(count):
    h = lambda m: scale * lam ** np.abs(m)
    i = np.arange(count)
    m = i[:, None] - i[None, :]
    own = near * (h(m + 1) - h(m - 1)) + far * (h(m + 2) - h(m - 2))
    high, low = host_halves(own)
    return np.concatenate([high, low, high], axis=1)


def y_operators(total, blocks):
    a = np.eye(total)
    b = np.zeros((total, total))
    for j in range(2, total - 2):
        a[j, j - 1] = a[j, j + 1] = third
        b[j, j + 1], b[j, j - 1], b[j, j + 2], b[j, j - 2] = near, -near, far, -far
    a[0, 1] = a[-1, -2] = 2.0
    b[0, :3] = -2.5, 2.0, 0.5
    b[-1, -3:] = -0.5, -2.0, 2.5
    for j in (1, total - 2):
        a[j, j - 1] = a[j, j + 1] = 0.25
        b[j, j + 1], b[j, j - 1] = 0.75, -0.75
    whole = np.linalg.solve(a, b)
    size = total // blocks
    out = []
    for g in range(blocks):
        own = whole[g * size : (g + 1) * size, g * size : (g + 1) * size].T
        high, low = host_halves(own)
        out.append(np.block([[high, low], [high, np.zeros_like(low)]]))
    return np.stack(out)


def power(n):
    size = jnp.exp(n.astype(f32) * log_lam)
    return jnp.where((n & 1) == 0, size, -size)


def x_message(f, msg, planes, at_right):
    depth, rows, lanes = f.shape
    k = lax.broadcasted_iota(jnp.int32, (rows, lanes), 0)
    weights = jnp.where(at_right, gamma * power(rows - k), -gamma * power(k + 1))
    msg[0, planes] = jnp.sum(f * weights[None], axis=1)
    msg[1, planes] = jnp.where(at_right, edge * f[:, rows - 1, :], -edge * f[:, 0, :])


def y_messages(fields, msg_c, msg_d):
    _, depth, rows, lanes = fields.shape
    even_y = lax.rem(lax.axis_index("gy"), 2) == 0
    j = lax.broadcasted_iota(jnp.int32, (8, lanes), 1)
    row = lax.broadcasted_iota(jnp.int32, (8, lanes), 0)
    odd = (row & 1) == 1
    y_right = jnp.where(odd, jnp.where(j == lanes - 1, edge, 0.0), gamma * power(lanes - j))
    y_left = jnp.where(odd, jnp.where(j == 0, -edge, 0.0), -gamma * power(j + 1))
    high, low = halves(jnp.where((row < 2) == even_y, y_right, y_left))
    both = jnp.concatenate([high, low], axis=0)
    nt = (((1,), (1,)), ((), ()))
    for i in range(4):
        fh, fl = halves(fields[i].reshape(depth * rows, lanes))
        top = lax.dot_general(both, fh, nt, preferred_element_type=f32)
        rest = lax.dot_general(both, fl, nt, preferred_element_type=f32)
        sums = top[0:8] + top[8:16] + rest[0:8]
        for b in range(depth * rows // lanes):
            part = sums[:, b * lanes : (b + 1) * lanes]
            msg_c[pl.ds(8 * b + 2 * i, 2), :] = part[0:2]
            msg_d[pl.ds(8 * b + 2 * i, 2), :] = part[2:4]


def edges_kernel(u, v, w, p, fields, chip, far_side, early_c, early_d, sems):
    depth, rows, lanes = u.shape
    piece = depth // pieces
    copies = [
        [
            pltpu.make_async_copy(
                s.at[pl.ds(n * piece, piece)],
                fields.at[i, pl.ds(n * piece, piece)],
                sems.at[i * pieces + n],
            )
            for n in range(pieces)
        ]
        for i, s in enumerate((u, v, w, p))
    ]
    for field in copies:
        for c in field:
            c.start()
    gx = lax.axis_index("gx")
    even_x = lax.rem(gx, 2) == 0
    early_d[...] = jnp.zeros_like(early_d)
    for i in range(4):
        for n in range(pieces):
            copies[i][n].wait()
            f = fields[i, pl.ds(n * piece, piece)]
            planes = pl.ds(n * piece, piece)
            x_message(f, chip.at[i], planes, even_x)
            x_message(f, far_side.at[i], planes, jnp.logical_not(even_x))

    @pl.when(gx < 2)
    def _():
        early_c[...] = jnp.zeros_like(early_c)
        y_messages(fields, early_c, early_d)

    @pl.when(gx >= 2)
    def _():
        early_c[...] = chip[...].reshape(early_c.shape)


def late_kernel(fields, chip, early_c, early_d, late_c, late_d):
    @pl.when(lax.axis_index("gx") < 2)
    def _():
        late_c[...] = chip[...].reshape(late_c.shape)
        late_d[...] = jnp.zeros_like(late_d)

    @pl.when(lax.axis_index("gx") >= 2)
    def _():
        y_messages(fields, late_c, late_d)


def own_kernel(fields, wx, wy_all, lorentz, lz_o, vx_o, vy_o, vz_o, dv_o, lx_s, ly_s, sems):
    _, depth, rows, lanes = fields.shape
    u, v, w, p = range(4)
    wy = wy_all.at[lax.axis_index("gy")]

    def dz(i, k):
        at = lambda s: fields[i, (k + s) & (depth - 1)]
        return (
            0.75 * (at(1) - at(-1)) - 0.15 * (at(2) - at(-2)) + (1.0 / 60.0) * (at(3) - at(-3))
        )


    @pl.loop(0, depth, step=own_step)
    def _(start):
        for n in range(own_step):
            k = start + n
            jz = by * fields[u, k] - bx * fields[v, k] - dz(p, k)
            lx_s[k] = -by * jz
            ly_s[k] = bx * jz

    put_x = pltpu.make_async_copy(lx_s, lorentz.at[0], sems.at[0])
    put_y = pltpu.make_async_copy(ly_s, lorentz.at[1], sems.at[1])
    put_x.start()
    put_y.start()
    def plane(k):
        split = [halves(fields[i, k]) for i in range(4)]
        highs = jnp.concatenate([s[0] for s in split], axis=0)
        lows = jnp.concatenate([s[1] for s in split], axis=0)
        y = jnp.dot(jnp.concatenate([highs, lows], axis=1), wy[...], preferred_element_type=f32)
        y = y[:, :lanes] + y[:, lanes:]
        wide_h = jnp.concatenate([s[0] for s in split], axis=1)
        wide_l = jnp.concatenate([s[1] for s in split], axis=1)
        x = jnp.dot(
            wx[...], jnp.concatenate([wide_h, wide_h, wide_l], axis=0), preferred_element_type=f32
        )
        yd = lambda i: y[i * rows : (i + 1) * rows]
        xd = lambda i: x[:, i * lanes : (i + 1) * lanes]
        lz_o[k] = bx * yd(p) - by * xd(p) - fields[w, k]
        vx_o[k] = yd(w) - dz(v, k)
        vy_o[k] = dz(u, k) - xd(w)
        vz_o[k] = xd(v) - yd(u)
        dv_o[k] = xd(u) + yd(v) + dz(w, k)

    @pl.loop(0, depth, step=own_step)
    def _(start):
        for n in range(own_step):
            plane(start + n)

    put_x.wait()
    put_y.wait()


def hold_kernel(message, held):
    pass


def y_spread(lanes, line):
    out = []
    j = np.arange(lanes)
    for g in range(line):
        table = np.zeros((16, 4, lanes))
        for side in range(2):
            from_left = (side == 1) == (g % 2 == 0)
            if (from_left and g == 0) or (not from_left and g == line - 1):
                continue
            away = j if from_left else lanes - 1 - j
            for field, (target, factor) in enumerate(((2, -1.0), (3, 1.0), (1, 1.0), (0, bx))):
                table[8 * side + 2 * field, target] = factor * lam**away
                table[8 * side + 2 * field + 1, target] = factor * (away == 0)
        table = table.reshape(16, 4 * lanes)
        table[np.abs(table) < 1e-37] = 0.0
        high, low = host_halves(table)
        out.append(np.concatenate([high, high, low], axis=0))
    return np.stack(out)


def join_kernel(
    got_far, early_c, early_d, late_c, late_d, spread_all, lz, vx, vy, vz, dv, lorentz_in,
    lorentz, vorticity, divergence, lz_s, vx_s, vy_s, vz_s, dv_s, chip_s, got_c, got_d, sems
):
    depth, rows, lanes = lz.shape
    gx = lax.axis_index("gx")
    even_x = lax.rem(gx, 2) == 0
    first = gx < 2
    spread = spread_all[lax.axis_index("gy")]
    got_c[...] = jnp.where(first, early_c[: got_c.shape[0]], late_c[: got_c.shape[0]])
    got_d[...] = jnp.where(first, early_d[...], late_d[...])
    chip_s[...] = jnp.where(first, late_c[...], early_c[...])
    i = lax.broadcasted_iota(jnp.int32, (rows, lanes), 0)
    fall_l, fall_r = power(i), power(rows - 1 - i)
    fall_chip = jnp.where(even_x, fall_r, fall_l)
    fall_far = jnp.where(even_x, fall_l, fall_r)
    sub = lax.broadcasted_iota(jnp.int32, (8, lanes), 0)
    low_far = jnp.where(jnp.logical_and(sub == 0, even_x), 1.0, 0.0)
    low_chip = jnp.where(jnp.logical_and(sub == 0, jnp.logical_not(even_x)), 1.0, 0.0)
    high_far = jnp.where(jnp.logical_and(sub == 7, jnp.logical_not(even_x)), 1.0, 0.0)
    high_chip = jnp.where(jnp.logical_and(sub == 7, even_x), 1.0, 0.0)

    def xc(f, k):
        at = lambda ref, kind: ref[pl.ds((2 * f + kind) * depth + k, 1), :]
        c = fall_far * at(got_far, 0) + fall_chip * at(chip_s, 0)
        far_e, chip_e = at(got_far, 1), at(chip_s, 1)
        head = c[:8] + low_far * far_e + low_chip * chip_e
        tail = c[rows - 8 :] + high_far * far_e + high_chip * chip_e
        return jnp.concatenate([head, c[8 : rows - 8], tail], axis=0)

    per = lanes // rows
    tn = (((0,), (0,)), ((), ()))
    targets = (
        (lz_s, lorentz.at[2]),
        (vx_s, vorticity.at[0]),
        (vy_s, vorticity.at[1]),
        (vz_s, vorticity.at[2]),
        (dv_s, divergence),
    )

    def puts(first_plane, last_plane):
        planes = pl.ds(first_plane, last_plane - first_plane)
        return [
            pltpu.make_async_copy(s.at[planes], d.at[planes], sems.at[n])
            for n, (s, d) in enumerate(targets)
        ]

    def group(first_plane, last_plane):
        for k in range(first_plane, last_plane):
            q = k % per
            if q == 0 or k == first_plane:
                rows_of = pl.ds(k // per * 8, 8)
                got = [m[rows_of, :] for m in (got_c, got_d)]
                high, low = halves(jnp.concatenate(got, axis=0))
                sums = jnp.concatenate([high, low, high], axis=0)
                yc = lax.dot_general(sums, spread, tn, preferred_element_type=f32)
            part = lambda t: yc[q * rows : (q + 1) * rows, t * lanes : (t + 1) * lanes]
            lz_s[k] = lz[k] + part(0) - by * xc(3, k)
            vx_s[k] = vx[k] + part(1)
            vy_s[k] = vy[k] - xc(2, k)
            vz_s[k] = vz[k] + part(2) + xc(1, k)
            dv_s[k] = dv[k] + part(3) + xc(0, k)
        for c in puts(first_plane, last_plane):
            c.start()

    start = 0
    for count in join_groups:
        pl.when(gx >= 0)(functools.partial(group, start, start + count))
        start += count
    for c in puts(0, depth):
        c.wait()


def local(wx, wy, spread, ring, line, u, v, w, p):
    depth, rows, lanes = u.shape
    block = (depth, rows, lanes)
    vmem = pl.BlockSpec(memory_space=pltpu.VMEM)
    anywhere = pl.BlockSpec(memory_space=pl.ANY)
    params = pltpu.CompilerParams(vmem_limit_bytes=24 * 2**20)
    keep = lambda x: pltpu.with_memory_space_constraint(x, pltpu.VMEM)
    stay = lambda x: pltpu.with_memory_space_constraint(x, pltpu.HBM)
    size = 4 * depth * rows * lanes
    cost = lambda flops, moved: pl.CostEstimate(
        flops=flops * size, bytes_accessed=moved * size, transcendentals=0
    )
    wx, wy, spread = (keep(jnp.asarray(t)) for t in (wx, wy, spread))
    msg = pltpu.VMEM((8 * depth, lanes), f32)
    x_msg = pltpu.VMEM((4, 2, depth, lanes), f32)
    half = pltpu.VMEM((4 * depth, lanes), f32)

    def over_chips(column):
        return [
            (i * line + j, column(i, j)[0] * line + column(i, j)[1])
            for i in range(ring)
            for j in range(line)
        ]

    mate = lambda i, j: (i ^ 1, j)
    y_one = lambda i, j: (i, j ^ 1)
    y_two = lambda i, j: (i, (j + 1) % line if j % 2 else (j - 1) % line)
    first = lambda a, b: over_chips(lambda i, j: a(i, j) if i < 2 else b(i, j))
    both = ("gx", "gy")

    fields, chip, far_side, early_c, early_d = pl.pallas_call(
        edges_kernel,
        name="edge_sums",
        out_shape=(pltpu.VMEM((4,) + block, f32), x_msg, x_msg, msg, half),
        in_specs=[anywhere] * 4,
        out_specs=(vmem,) * 5,
        scratch_shapes=[pltpu.SemaphoreType.DMA((4 * pieces,))],
        compiler_params=params,
        cost_estimate=cost(1, 1),
    )(*(stay(x) for x in (u, v, w, p)))
    early_c = lax.ppermute(early_c, both, first(y_one, mate))
    early_d = lax.ppermute(early_d, both, first(y_two, mate))

    far_side = pl.pallas_call(
        hold_kernel,
        name="hold",
        out_shape=x_msg,
        in_specs=[vmem],
        out_specs=vmem,
        input_output_aliases={0: 0},
        compiler_params=params,
        cost_estimate=cost(1, 1),
    )(keep(far_side))
    got_far = lax.ppermute(
        far_side, "gx", [(i, (i + 1) % ring if i % 2 else (i - 1) % ring) for i in range(ring)]
    )

    late_c, late_d = pl.pallas_call(
        late_kernel,
        name="y_sums",
        out_shape=(msg, half),
        in_specs=[vmem, vmem, anywhere, anywhere],
        out_specs=(vmem,) * 2,
        compiler_params=params,
        cost_estimate=cost(1, 1),
    )(*(keep(x) for x in (fields, chip, early_c, early_d)))
    late_c = lax.ppermute(late_c, both, first(mate, y_one))
    late_d = lax.ppermute(late_d, both, first(mate, y_two))

    lorentz, *part = pl.pallas_call(
        own_kernel,
        name="own_block",
        out_shape=(jax.ShapeDtypeStruct((3,) + block, f32),) + (pltpu.VMEM(block, f32),) * 5,
        in_specs=[vmem] * 3,
        out_specs=(anywhere,) + (vmem,) * 5,
        scratch_shapes=[
            pltpu.VMEM(block, f32),
            pltpu.VMEM(block, f32),
            pltpu.SemaphoreType.DMA((2,)),
        ],
        compiler_params=params,
        cost_estimate=cost(4000, 12),
    )(keep(fields), wx, wy)

    got_far = got_far.reshape(msg.shape)
    return pl.pallas_call(
        join_kernel,
        name="join",
        out_shape=(
            jax.ShapeDtypeStruct((3,) + block, f32),
            jax.ShapeDtypeStruct((3,) + block, f32),
            jax.ShapeDtypeStruct(block, f32),
        ),
        in_specs=[vmem] * 11 + [anywhere],
        out_specs=(anywhere,) * 3,
        scratch_shapes=[pltpu.VMEM(block, f32)] * 5
        + [pltpu.VMEM(msg.shape, f32), pltpu.VMEM(half.shape, f32), pltpu.VMEM(half.shape, f32)]
        + [pltpu.SemaphoreType.DMA((5,))],
        input_output_aliases={11: 0},
        compiler_params=params,
        cost_estimate=cost(30, 12),
    )(
        *(keep(x) for x in (got_far, early_c, early_d, late_c, late_d)),
        spread,
        *(keep(x) for x in part),
        lorentz,
    )


def solution(mesh):
    ring, line = mesh.shape["gx"], mesh.shape["gy"]
    cells = P(None, "gx", "gy")
    stacked = P(None, None, "gx", "gy")
    wx = x_operator(4096 // ring)
    wy = y_operators(512, line)
    spread = y_spread(512 // line, line)
    return jax.shard_map(
        functools.partial(local, wx, wy, spread, ring, line),
        mesh=mesh,
        in_specs=(cells,) * 4,
        out_specs=(stacked, stacked, cells),
        check_vma=False,
    )
```

```python
import functools
import math

import jax
import jax.numpy as jnp
import ml_dtypes
import numpy as np
from jax import lax
from jax.experimental import pallas as pl
from jax.experimental.pallas import tpu as pltpu
from jax.sharding import PartitionSpec as P

third = 1.0 / 3.0
near = 7.0 / 9.0
far = 1.0 / 36.0
bx = 0.6
by = 0.8

lam = (-3.0 + math.sqrt(5.0)) / 2.0
scale = 1.0 / (1.0 + 2.0 * third * lam)
log_lam = math.log(-lam)
gamma = scale * (near * (lam - 1.0 / lam) + far * (lam**2 - lam**-2))
edge = scale * (near * (lam**2 - 1.0) + far * (lam**3 - lam)) - gamma * lam

f32 = jnp.float32
bf16 = jnp.bfloat16
pieces = 1
own_step = 8
join_groups = (2, 2, 2, 2, 2, 2, 2, 2)


def halves(values):
    high = values.astype(bf16)
    return high, (values - high.astype(f32)).astype(bf16)


def host_halves(values):
    values = values.astype(np.float32)
    high = values.astype(ml_dtypes.bfloat16)
    low = (values - high.astype(np.float32)).astype(ml_dtypes.bfloat16)
    return high, low


def x_operator(count):
    h = lambda m: scale * lam ** np.abs(m)
    i = np.arange(count)
    m = i[:, None] - i[None, :]
    own = near * (h(m + 1) - h(m - 1)) + far * (h(m + 2) - h(m - 2))
    high, low = host_halves(own)
    return np.concatenate([high, low, high], axis=1)


def y_operators(total, blocks):
    a = np.eye(total)
    b = np.zeros((total, total))
    for j in range(2, total - 2):
        a[j, j - 1] = a[j, j + 1] = third
        b[j, j + 1], b[j, j - 1], b[j, j + 2], b[j, j - 2] = near, -near, far, -far
    a[0, 1] = a[-1, -2] = 2.0
    b[0, :3] = -2.5, 2.0, 0.5
    b[-1, -3:] = -0.5, -2.0, 2.5
    for j in (1, total - 2):
        a[j, j - 1] = a[j, j + 1] = 0.25
        b[j, j + 1], b[j, j - 1] = 0.75, -0.75
    whole = np.linalg.solve(a, b)
    size = total // blocks
    out = []
    for g in range(blocks):
        own = whole[g * size : (g + 1) * size, g * size : (g + 1) * size].T
        high, low = host_halves(own)
        out.append(np.block([[high, low], [high, np.zeros_like(low)]]))
    return np.stack(out)


def power(n):
    size = jnp.exp(n.astype(f32) * log_lam)
    return jnp.where((n & 1) == 0, size, -size)


def x_message(f, msg, planes, at_right):
    depth, rows, lanes = f.shape
    k = lax.broadcasted_iota(jnp.int32, (rows, lanes), 0)
    weights = jnp.where(at_right, gamma * power(rows - k), -gamma * power(k + 1))
    msg[0, planes] = jnp.sum(f * weights[None], axis=1)
    msg[1, planes] = jnp.where(at_right, edge * f[:, rows - 1, :], -edge * f[:, 0, :])


def y_messages(fields, msg_c, msg_d):
    _, depth, rows, lanes = fields.shape
    even_y = lax.rem(lax.axis_index("gy"), 2) == 0
    j = lax.broadcasted_iota(jnp.int32, (8, lanes), 1)
    row = lax.broadcasted_iota(jnp.int32, (8, lanes), 0)
    odd = (row & 1) == 1
    y_right = jnp.where(odd, jnp.where(j == lanes - 1, edge, 0.0), gamma * power(lanes - j))
    y_left = jnp.where(odd, jnp.where(j == 0, -edge, 0.0), -gamma * power(j + 1))
    high, low = halves(jnp.where((row < 2) == even_y, y_right, y_left))
    both = jnp.concatenate([high, low], axis=0)
    nt = (((1,), (1,)), ((), ()))
    for i in range(4):
        fh, fl = halves(fields[i].reshape(depth * rows, lanes))
        top = lax.dot_general(both, fh, nt, preferred_element_type=f32)
        rest = lax.dot_general(both, fl, nt, preferred_element_type=f32)
        sums = top[0:8] + top[8:16] + rest[0:8]
        for b in range(depth * rows // lanes):
            part = sums[:, b * lanes : (b + 1) * lanes]
            msg_c[pl.ds(8 * b + 2 * i, 2), :] = part[0:2]
            msg_d[pl.ds(8 * b + 2 * i, 2), :] = part[2:4]


def edges_kernel(u, v, w, p, fields, chip, far_side, early_c, early_d, sems):
    depth, rows, lanes = u.shape
    piece = depth // pieces
    copies = [
        [
            pltpu.make_async_copy(
                s.at[pl.ds(n * piece, piece)],
                fields.at[i, pl.ds(n * piece, piece)],
                sems.at[i * pieces + n],
            )
            for n in range(pieces)
        ]
        for i, s in enumerate((u, v, w, p))
    ]
    for field in copies:
        for c in field:
            c.start()
    gx = lax.axis_index("gx")
    even_x = lax.rem(gx, 2) == 0
    early_d[...] = jnp.zeros_like(early_d)
    for i in range(4):
        for n in range(pieces):
            copies[i][n].wait()
            f = fields[i, pl.ds(n * piece, piece)]
            planes = pl.ds(n * piece, piece)
            x_message(f, chip.at[i], planes, even_x)
            x_message(f, far_side.at[i], planes, jnp.logical_not(even_x))

    @pl.when(gx < 2)
    def _():
        early_c[...] = jnp.zeros_like(early_c)
        y_messages(fields, early_c, early_d)

    @pl.when(gx >= 2)
    def _():
        early_c[...] = chip[...].reshape(early_c.shape)


def late_kernel(fields, chip, part, late_c, late_d):
    @pl.when(lax.axis_index("gx") < 2)
    def _():
        late_c[...] = chip[...].reshape(late_c.shape)
        late_d[...] = jnp.zeros_like(late_d)

    @pl.when(lax.axis_index("gx") >= 2)
    def _():
        y_messages(fields, late_c, late_d)


def own_block(fields, wx, wy_all, lorentz, lz_o, vx_o, vy_o, vz_o, dv_o, lx_s, ly_s, sems):
    _, depth, rows, lanes = fields.shape
    u, v, w, p = range(4)
    wy = wy_all.at[lax.axis_index("gy")]

    def dz(i, k):
        at = lambda s: fields[i, (k + s) & (depth - 1)]
        return (
            0.75 * (at(1) - at(-1)) - 0.15 * (at(2) - at(-2)) + (1.0 / 60.0) * (at(3) - at(-3))
        )


    @pl.loop(0, depth, step=own_step)
    def _(start):
        for n in range(own_step):
            k = start + n
            jz = by * fields[u, k] - bx * fields[v, k] - dz(p, k)
            lx_s[k] = -by * jz
            ly_s[k] = bx * jz

    put_x = pltpu.make_async_copy(lx_s, lorentz.at[0], sems.at[0])
    put_y = pltpu.make_async_copy(ly_s, lorentz.at[1], sems.at[1])
    put_x.start()
    put_y.start()
    def plane(k):
        split = [halves(fields[i, k]) for i in range(4)]
        highs = jnp.concatenate([s[0] for s in split], axis=0)
        lows = jnp.concatenate([s[1] for s in split], axis=0)
        y = jnp.dot(jnp.concatenate([highs, lows], axis=1), wy[...], preferred_element_type=f32)
        y = y[:, :lanes] + y[:, lanes:]
        wide_h = jnp.concatenate([s[0] for s in split], axis=1)
        wide_l = jnp.concatenate([s[1] for s in split], axis=1)
        x = jnp.dot(
            wx[...], jnp.concatenate([wide_h, wide_h, wide_l], axis=0), preferred_element_type=f32
        )
        yd = lambda i: y[i * rows : (i + 1) * rows]
        xd = lambda i: x[:, i * lanes : (i + 1) * lanes]
        lz_o[k] = bx * yd(p) - by * xd(p) - fields[w, k]
        vx_o[k] = yd(w) - dz(v, k)
        vy_o[k] = dz(u, k) - xd(w)
        vz_o[k] = xd(v) - yd(u)
        dv_o[k] = xd(u) + yd(v) + dz(w, k)

    @pl.loop(0, depth, step=own_step)
    def _(start):
        for n in range(own_step):
            plane(start + n)

    put_x.wait()
    put_y.wait()


def waiting_kernel(fields, wx, wy_all, early_c, early_d, *rest):
    @pl.when(lax.axis_index("gx") == 1)
    def _():
        own_block(fields, wx, wy_all, *rest)


def rest_kernel(fields, wx, wy_all, *rest):
    @pl.when(lax.axis_index("gx") != 1)
    def _():
        own_block(fields, wx, wy_all, *rest[6:])


def hold_kernel(message, held):
    pass


def y_spread(lanes, line):
    out = []
    j = np.arange(lanes)
    for g in range(line):
        table = np.zeros((16, 4, lanes))
        for side in range(2):
            from_left = (side == 1) == (g % 2 == 0)
            if (from_left and g == 0) or (not from_left and g == line - 1):
                continue
            away = j if from_left else lanes - 1 - j
            for field, (target, factor) in enumerate(((2, -1.0), (3, 1.0), (1, 1.0), (0, bx))):
                table[8 * side + 2 * field, target] = factor * lam**away
                table[8 * side + 2 * field + 1, target] = factor * (away == 0)
        table = table.reshape(16, 4 * lanes)
        table[np.abs(table) < 1e-37] = 0.0
        high, low = host_halves(table)
        out.append(np.concatenate([high, high, low], axis=0))
    return np.stack(out)


def join_kernel(
    got_far, early_c, early_d, late_c, late_d, spread_all, lz, vx, vy, vz, dv, lorentz_in,
    lorentz, vorticity, divergence, lz_s, vx_s, vy_s, vz_s, dv_s, chip_s, got_c, got_d, sems
):
    depth, rows, lanes = lz.shape
    gx = lax.axis_index("gx")
    even_x = lax.rem(gx, 2) == 0
    first = gx < 2
    spread = spread_all[lax.axis_index("gy")]
    got_c[...] = jnp.where(first, early_c[: got_c.shape[0]], late_c[: got_c.shape[0]])
    got_d[...] = jnp.where(first, early_d[...], late_d[...])
    chip_s[...] = jnp.where(first, late_c[...], early_c[...])
    i = lax.broadcasted_iota(jnp.int32, (rows, lanes), 0)
    fall_l, fall_r = power(i), power(rows - 1 - i)
    fall_chip = jnp.where(even_x, fall_r, fall_l)
    fall_far = jnp.where(even_x, fall_l, fall_r)
    sub = lax.broadcasted_iota(jnp.int32, (8, lanes), 0)
    low_far = jnp.where(jnp.logical_and(sub == 0, even_x), 1.0, 0.0)
    low_chip = jnp.where(jnp.logical_and(sub == 0, jnp.logical_not(even_x)), 1.0, 0.0)
    high_far = jnp.where(jnp.logical_and(sub == 7, jnp.logical_not(even_x)), 1.0, 0.0)
    high_chip = jnp.where(jnp.logical_and(sub == 7, even_x), 1.0, 0.0)

    def xc(f, k):
        at = lambda ref, kind: ref[pl.ds((2 * f + kind) * depth + k, 1), :]
        c = fall_far * at(got_far, 0) + fall_chip * at(chip_s, 0)
        far_e, chip_e = at(got_far, 1), at(chip_s, 1)
        head = c[:8] + low_far * far_e + low_chip * chip_e
        tail = c[rows - 8 :] + high_far * far_e + high_chip * chip_e
        return jnp.concatenate([head, c[8 : rows - 8], tail], axis=0)

    per = lanes // rows
    tn = (((0,), (0,)), ((), ()))
    targets = (
        (lz_s, lorentz.at[2]),
        (vx_s, vorticity.at[0]),
        (vy_s, vorticity.at[1]),
        (vz_s, vorticity.at[2]),
        (dv_s, divergence),
    )

    def puts(first_plane, last_plane):
        planes = pl.ds(first_plane, last_plane - first_plane)
        return [
            pltpu.make_async_copy(s.at[planes], d.at[planes], sems.at[n])
            for n, (s, d) in enumerate(targets)
        ]

    def group(first_plane, last_plane):
        for k in range(first_plane, last_plane):
            q = k % per
            if q == 0 or k == first_plane:
                rows_of = pl.ds(k // per * 8, 8)
                got = [m[rows_of, :] for m in (got_c, got_d)]
                high, low = halves(jnp.concatenate(got, axis=0))
                sums = jnp.concatenate([high, low, high], axis=0)
                yc = lax.dot_general(sums, spread, tn, preferred_element_type=f32)
            part = lambda t: yc[q * rows : (q + 1) * rows, t * lanes : (t + 1) * lanes]
            lz_s[k] = lz[k] + part(0) - by * xc(3, k)
            vx_s[k] = vx[k] + part(1)
            vy_s[k] = vy[k] - xc(2, k)
            vz_s[k] = vz[k] + part(2) + xc(1, k)
            dv_s[k] = dv[k] + part(3) + xc(0, k)
        for c in puts(first_plane, last_plane):
            c.start()

    start = 0
    for count in join_groups:
        pl.when(gx >= 0)(functools.partial(group, start, start + count))
        start += count
    for c in puts(0, depth):
        c.wait()


def local(wx, wy, spread, ring, line, u, v, w, p):
    depth, rows, lanes = u.shape
    block = (depth, rows, lanes)
    vmem = pl.BlockSpec(memory_space=pltpu.VMEM)
    anywhere = pl.BlockSpec(memory_space=pl.ANY)
    params = pltpu.CompilerParams(vmem_limit_bytes=24 * 2**20)
    keep = lambda x: pltpu.with_memory_space_constraint(x, pltpu.VMEM)
    stay = lambda x: pltpu.with_memory_space_constraint(x, pltpu.HBM)
    size = 4 * depth * rows * lanes
    cost = lambda flops, moved: pl.CostEstimate(
        flops=flops * size, bytes_accessed=moved * size, transcendentals=0
    )
    wx, wy, spread = (keep(jnp.asarray(t)) for t in (wx, wy, spread))
    msg = pltpu.VMEM((8 * depth, lanes), f32)
    x_msg = pltpu.VMEM((4, 2, depth, lanes), f32)
    half = pltpu.VMEM((4 * depth, lanes), f32)

    def over_chips(column):
        return [
            (i * line + j, column(i, j)[0] * line + column(i, j)[1])
            for i in range(ring)
            for j in range(line)
        ]

    mate = lambda i, j: (i ^ 1, j)
    y_one = lambda i, j: (i, j ^ 1)
    y_two = lambda i, j: (i, (j + 1) % line if j % 2 else (j - 1) % line)
    first = lambda a, b: over_chips(lambda i, j: a(i, j) if i < 2 else b(i, j))
    both = ("gx", "gy")

    fields, chip, far_side, early_c, early_d = pl.pallas_call(
        edges_kernel,
        name="edge_sums",
        out_shape=(pltpu.VMEM((4,) + block, f32), x_msg, x_msg, msg, half),
        in_specs=[anywhere] * 4,
        out_specs=(vmem,) * 5,
        scratch_shapes=[pltpu.SemaphoreType.DMA((4 * pieces,))],
        compiler_params=params,
        cost_estimate=cost(20000, 12),
    )(*(stay(x) for x in (u, v, w, p)))
    early_c = lax.ppermute(early_c, both, first(y_one, mate))
    early_d = lax.ppermute(early_d, both, first(y_two, mate))

    far_side = pl.pallas_call(
        hold_kernel,
        name="hold",
        out_shape=x_msg,
        in_specs=[vmem],
        out_specs=vmem,
        input_output_aliases={0: 0},
        compiler_params=params,
        cost_estimate=cost(20000, 12),
    )(keep(far_side))
    got_far = lax.ppermute(
        far_side, "gx", [(i, (i + 1) % ring if i % 2 else (i - 1) % ring) for i in range(ring)]
    )

    parts = (jax.ShapeDtypeStruct((3,) + block, f32),) + (pltpu.VMEM(block, f32),) * 5
    scratch = [
        pltpu.VMEM(block, f32),
        pltpu.VMEM(block, f32),
        pltpu.SemaphoreType.DMA((2,)),
    ]
    lorentz, *part = pl.pallas_call(
        waiting_kernel,
        name="own_block_column_one",
        out_shape=parts,
        in_specs=[vmem] * 3 + [anywhere] * 2,
        out_specs=(anywhere,) + (vmem,) * 5,
        scratch_shapes=scratch,
        compiler_params=params,
        cost_estimate=cost(1, 1),
    )(keep(fields), wx, wy, keep(early_c), keep(early_d))

    late_c, late_d = pl.pallas_call(
        late_kernel,
        name="y_sums",
        out_shape=(msg, half),
        in_specs=[vmem, vmem, anywhere],
        out_specs=(vmem,) * 2,
        compiler_params=params,
        cost_estimate=cost(1, 1),
    )(*(keep(x) for x in (fields, chip, part[0])))
    late_c = lax.ppermute(late_c, both, first(mate, y_one))
    late_d = lax.ppermute(late_d, both, first(mate, y_two))

    lorentz, *part = pl.pallas_call(
        rest_kernel,
        name="own_block",
        out_shape=parts,
        in_specs=[vmem] * 3 + [anywhere] + [vmem] * 5,
        out_specs=(anywhere,) + (vmem,) * 5,
        scratch_shapes=scratch,
        input_output_aliases={i + 3: i for i in range(6)},
        compiler_params=params,
        cost_estimate=cost(100, 12),
    )(keep(fields), wx, wy, lorentz, *(keep(x) for x in part))

    got_far = got_far.reshape(msg.shape)
    return pl.pallas_call(
        join_kernel,
        name="join",
        out_shape=(
            jax.ShapeDtypeStruct((3,) + block, f32),
            jax.ShapeDtypeStruct((3,) + block, f32),
            jax.ShapeDtypeStruct(block, f32),
        ),
        in_specs=[vmem] * 11 + [anywhere],
        out_specs=(anywhere,) * 3,
        scratch_shapes=[pltpu.VMEM(block, f32)] * 5
        + [pltpu.VMEM(msg.shape, f32), pltpu.VMEM(half.shape, f32), pltpu.VMEM(half.shape, f32)]
        + [pltpu.SemaphoreType.DMA((5,))],
        input_output_aliases={11: 0},
        compiler_params=params,
        cost_estimate=cost(10, 10),
    )(
        *(keep(x) for x in (got_far, early_c, early_d, late_c, late_d)),
        spread,
        *(keep(x) for x in part),
        lorentz,
    )


def solution(mesh):
    ring, line = mesh.shape["gx"], mesh.shape["gy"]
    cells = P(None, "gx", "gy")
    stacked = P(None, None, "gx", "gy")
    wx = x_operator(4096 // ring)
    wy = y_operators(512, line)
    spread = y_spread(512 // line, line)
    return jax.shard_map(
        functools.partial(local, wx, wy, spread, ring, line),
        mesh=mesh,
        in_specs=(cells,) * 4,
        out_specs=(stacked, stacked, cells),
        check_vma=False,
    )
```

```python
import functools
import math

import jax
import jax.numpy as jnp
import ml_dtypes
import numpy as np
from jax import lax
from jax.experimental import pallas as pl
from jax.experimental.pallas import tpu as pltpu
from jax.sharding import PartitionSpec as P

third = 1.0 / 3.0
near = 7.0 / 9.0
far = 1.0 / 36.0
bx = 0.6
by = 0.8

lam = (-3.0 + math.sqrt(5.0)) / 2.0
scale = 1.0 / (1.0 + 2.0 * third * lam)
log_lam = math.log(-lam)
gamma = scale * (near * (lam - 1.0 / lam) + far * (lam**2 - lam**-2))
edge = scale * (near * (lam**2 - 1.0) + far * (lam**3 - lam)) - gamma * lam

f32 = jnp.float32
bf16 = jnp.bfloat16
pieces = 1
own_step = 8
join_groups = (2, 2, 2, 2, 2, 2, 2, 2)


def halves(values):
    high = values.astype(bf16)
    return high, (values - high.astype(f32)).astype(bf16)


def host_halves(values):
    values = values.astype(np.float32)
    high = values.astype(ml_dtypes.bfloat16)
    low = (values - high.astype(np.float32)).astype(ml_dtypes.bfloat16)
    return high, low


def x_operator(count):
    h = lambda m: scale * lam ** np.abs(m)
    i = np.arange(count)
    m = i[:, None] - i[None, :]
    own = near * (h(m + 1) - h(m - 1)) + far * (h(m + 2) - h(m - 2))
    high, low = host_halves(own)
    return np.concatenate([high, low, high], axis=1)


def y_operators(total, blocks):
    a = np.eye(total)
    b = np.zeros((total, total))
    for j in range(2, total - 2):
        a[j, j - 1] = a[j, j + 1] = third
        b[j, j + 1], b[j, j - 1], b[j, j + 2], b[j, j - 2] = near, -near, far, -far
    a[0, 1] = a[-1, -2] = 2.0
    b[0, :3] = -2.5, 2.0, 0.5
    b[-1, -3:] = -0.5, -2.0, 2.5
    for j in (1, total - 2):
        a[j, j - 1] = a[j, j + 1] = 0.25
        b[j, j + 1], b[j, j - 1] = 0.75, -0.75
    whole = np.linalg.solve(a, b)
    size = total // blocks
    out = []
    for g in range(blocks):
        own = whole[g * size : (g + 1) * size, g * size : (g + 1) * size].T
        high, low = host_halves(own)
        out.append(np.block([[high, low], [high, np.zeros_like(low)]]))
    return np.stack(out)


def power(n):
    size = jnp.exp(n.astype(f32) * log_lam)
    return jnp.where((n & 1) == 0, size, -size)


def x_message(f, msg, planes, at_right):
    depth, rows, lanes = f.shape
    k = lax.broadcasted_iota(jnp.int32, (rows, lanes), 0)
    weights = jnp.where(at_right, gamma * power(rows - k), -gamma * power(k + 1))
    msg[0, planes] = jnp.sum(f * weights[None], axis=1)
    msg[1, planes] = jnp.where(at_right, edge * f[:, rows - 1, :], -edge * f[:, 0, :])


def y_messages(fields, msg_c, msg_d):
    _, depth, rows, lanes = fields.shape
    even_y = lax.rem(lax.axis_index("gy"), 2) == 0
    j = lax.broadcasted_iota(jnp.int32, (8, lanes), 1)
    row = lax.broadcasted_iota(jnp.int32, (8, lanes), 0)
    odd = (row & 1) == 1
    y_right = jnp.where(odd, jnp.where(j == lanes - 1, edge, 0.0), gamma * power(lanes - j))
    y_left = jnp.where(odd, jnp.where(j == 0, -edge, 0.0), -gamma * power(j + 1))
    high, low = halves(jnp.where((row < 2) == even_y, y_right, y_left))
    both = jnp.concatenate([high, low], axis=0)
    nt = (((1,), (1,)), ((), ()))
    for i in range(4):
        fh, fl = halves(fields[i].reshape(depth * rows, lanes))
        top = lax.dot_general(both, fh, nt, preferred_element_type=f32)
        rest = lax.dot_general(both, fl, nt, preferred_element_type=f32)
        sums = top[0:8] + top[8:16] + rest[0:8]
        for b in range(depth * rows // lanes):
            part = sums[:, b * lanes : (b + 1) * lanes]
            msg_c[pl.ds(8 * b + 2 * i, 2), :] = part[0:2]
            msg_d[pl.ds(8 * b + 2 * i, 2), :] = part[2:4]


def edges_kernel(u, v, w, p, fields, chip, far_side, early_c, early_d, sems):
    depth, rows, lanes = u.shape
    piece = depth // pieces
    copies = [
        [
            pltpu.make_async_copy(
                s.at[pl.ds(n * piece, piece)],
                fields.at[i, pl.ds(n * piece, piece)],
                sems.at[i * pieces + n],
            )
            for n in range(pieces)
        ]
        for i, s in enumerate((u, v, w, p))
    ]
    for field in copies:
        for c in field:
            c.start()
    gx = lax.axis_index("gx")
    even_x = lax.rem(gx, 2) == 0
    early_d[...] = jnp.zeros_like(early_d)
    for i in range(4):
        for n in range(pieces):
            copies[i][n].wait()
            f = fields[i, pl.ds(n * piece, piece)]
            planes = pl.ds(n * piece, piece)
            x_message(f, chip.at[i], planes, even_x)
            x_message(f, far_side.at[i], planes, jnp.logical_not(even_x))

    @pl.when(gx < 2)
    def _():
        early_c[...] = jnp.zeros_like(early_c)
        y_messages(fields, early_c, early_d)

    @pl.when(gx >= 2)
    def _():
        early_c[...] = chip[...].reshape(early_c.shape)


def late_kernel(fields, chip, part, late_c, late_d):
    @pl.when(lax.axis_index("gx") < 2)
    def _():
        late_c[...] = chip[...].reshape(late_c.shape)
        late_d[...] = jnp.zeros_like(late_d)

    @pl.when(lax.axis_index("gx") >= 2)
    def _():
        y_messages(fields, late_c, late_d)


def own_block(fields, wx, wy_all, lorentz, lz_o, vx_o, vy_o, vz_o, dv_o, lx_s, ly_s, sems):
    _, depth, rows, lanes = fields.shape
    u, v, w, p = range(4)
    wy = wy_all.at[lax.axis_index("gy")]

    def dz(i, k):
        at = lambda s: fields[i, (k + s) & (depth - 1)]
        return (
            0.75 * (at(1) - at(-1)) - 0.15 * (at(2) - at(-2)) + (1.0 / 60.0) * (at(3) - at(-3))
        )


    @pl.loop(0, depth, step=own_step)
    def _(start):
        for n in range(own_step):
            k = start + n
            jz = by * fields[u, k] - bx * fields[v, k] - dz(p, k)
            lx_s[k] = -by * jz
            ly_s[k] = bx * jz

    put_x = pltpu.make_async_copy(lx_s, lorentz.at[0], sems.at[0])
    put_y = pltpu.make_async_copy(ly_s, lorentz.at[1], sems.at[1])
    put_x.start()
    put_y.start()
    def plane(k):
        split = [halves(fields[i, k]) for i in range(4)]
        highs = jnp.concatenate([s[0] for s in split], axis=0)
        lows = jnp.concatenate([s[1] for s in split], axis=0)
        y = jnp.dot(jnp.concatenate([highs, lows], axis=1), wy[...], preferred_element_type=f32)
        y = y[:, :lanes] + y[:, lanes:]
        wide_h = jnp.concatenate([s[0] for s in split], axis=1)
        wide_l = jnp.concatenate([s[1] for s in split], axis=1)
        x = jnp.dot(
            wx[...], jnp.concatenate([wide_h, wide_h, wide_l], axis=0), preferred_element_type=f32
        )
        yd = lambda i: y[i * rows : (i + 1) * rows]
        xd = lambda i: x[:, i * lanes : (i + 1) * lanes]
        lz_o[k] = bx * yd(p) - by * xd(p) - fields[w, k]
        vx_o[k] = yd(w) - dz(v, k)
        vy_o[k] = dz(u, k) - xd(w)
        vz_o[k] = xd(v) - yd(u)
        dv_o[k] = xd(u) + yd(v) + dz(w, k)

    @pl.loop(0, depth, step=own_step)
    def _(start):
        for n in range(own_step):
            plane(start + n)

    put_x.wait()
    put_y.wait()


def waiting_kernel(fields, wx, wy_all, early_c, early_d, *rest):
    @pl.when(lax.axis_index("gx") == 1)
    def _():
        own_block(fields, wx, wy_all, *rest)


def rest_kernel(fields, wx, wy_all, *rest):
    @pl.when(lax.axis_index("gx") != 1)
    def _():
        own_block(fields, wx, wy_all, *rest[6:])


def hold_kernel(message, held):
    pass


def y_spread(lanes, line):
    out = []
    j = np.arange(lanes)
    for g in range(line):
        table = np.zeros((16, 4, lanes))
        for side in range(2):
            from_left = (side == 1) == (g % 2 == 0)
            if (from_left and g == 0) or (not from_left and g == line - 1):
                continue
            away = j if from_left else lanes - 1 - j
            for field, (target, factor) in enumerate(((2, -1.0), (3, 1.0), (1, 1.0), (0, bx))):
                table[8 * side + 2 * field, target] = factor * lam**away
                table[8 * side + 2 * field + 1, target] = factor * (away == 0)
        table = table.reshape(16, 4 * lanes)
        table[np.abs(table) < 1e-37] = 0.0
        high, low = host_halves(table)
        out.append(np.concatenate([high, high, low], axis=0))
    return np.stack(out)


def join_kernel(
    got_far, early_c, early_d, late_c, late_d, spread_all, lz, vx, vy, vz, dv, lorentz_in,
    lorentz, vorticity, divergence, lz_s, vx_s, vy_s, vz_s, dv_s, chip_s, got_c, got_d, sems
):
    depth, rows, lanes = lz.shape
    gx = lax.axis_index("gx")
    even_x = lax.rem(gx, 2) == 0
    first = gx < 2
    spread = spread_all[lax.axis_index("gy")]
    got_c[...] = jnp.where(first, early_c[: got_c.shape[0]], late_c[: got_c.shape[0]])
    got_d[...] = jnp.where(first, early_d[...], late_d[...])
    chip_s[...] = jnp.where(first, late_c[...], early_c[...])
    i = lax.broadcasted_iota(jnp.int32, (rows, lanes), 0)
    fall_l, fall_r = power(i), power(rows - 1 - i)
    fall_chip = jnp.where(even_x, fall_r, fall_l)
    fall_far = jnp.where(even_x, fall_l, fall_r)
    sub = lax.broadcasted_iota(jnp.int32, (8, lanes), 0)
    low_far = jnp.where(jnp.logical_and(sub == 0, even_x), 1.0, 0.0)
    low_chip = jnp.where(jnp.logical_and(sub == 0, jnp.logical_not(even_x)), 1.0, 0.0)
    high_far = jnp.where(jnp.logical_and(sub == 7, jnp.logical_not(even_x)), 1.0, 0.0)
    high_chip = jnp.where(jnp.logical_and(sub == 7, even_x), 1.0, 0.0)

    def xc(f, k):
        at = lambda ref, kind: ref[pl.ds((2 * f + kind) * depth + k, 1), :]
        c = fall_far * at(got_far, 0) + fall_chip * at(chip_s, 0)
        far_e, chip_e = at(got_far, 1), at(chip_s, 1)
        head = c[:8] + low_far * far_e + low_chip * chip_e
        tail = c[rows - 8 :] + high_far * far_e + high_chip * chip_e
        return jnp.concatenate([head, c[8 : rows - 8], tail], axis=0)

    per = lanes // rows
    tn = (((0,), (0,)), ((), ()))
    targets = (
        (lz_s, lorentz.at[2]),
        (vx_s, vorticity.at[0]),
        (vy_s, vorticity.at[1]),
        (vz_s, vorticity.at[2]),
        (dv_s, divergence),
    )

    def puts(first_plane, last_plane):
        planes = pl.ds(first_plane, last_plane - first_plane)
        return [
            pltpu.make_async_copy(s.at[planes], d.at[planes], sems.at[n])
            for n, (s, d) in enumerate(targets)
        ]

    def group(first_plane, last_plane):
        for k in range(first_plane, last_plane):
            q = k % per
            if q == 0 or k == first_plane:
                rows_of = pl.ds(k // per * 8, 8)
                got = [m[rows_of, :] for m in (got_c, got_d)]
                high, low = halves(jnp.concatenate(got, axis=0))
                sums = jnp.concatenate([high, low, high], axis=0)
                yc = lax.dot_general(sums, spread, tn, preferred_element_type=f32)
            part = lambda t: yc[q * rows : (q + 1) * rows, t * lanes : (t + 1) * lanes]
            lz_s[k] = lz[k] + part(0) - by * xc(3, k)
            vx_s[k] = vx[k] + part(1)
            vy_s[k] = vy[k] - xc(2, k)
            vz_s[k] = vz[k] + part(2) + xc(1, k)
            dv_s[k] = dv[k] + part(3) + xc(0, k)
        for c in puts(first_plane, last_plane):
            c.start()

    start = 0
    for count in join_groups:
        pl.when(gx >= 0)(functools.partial(group, start, start + count))
        start += count
    for c in puts(0, depth):
        c.wait()


def local(wx, wy, spread, ring, line, u, v, w, p):
    depth, rows, lanes = u.shape
    block = (depth, rows, lanes)
    vmem = pl.BlockSpec(memory_space=pltpu.VMEM)
    anywhere = pl.BlockSpec(memory_space=pl.ANY)
    params = pltpu.CompilerParams(vmem_limit_bytes=24 * 2**20)
    keep = lambda x: pltpu.with_memory_space_constraint(x, pltpu.VMEM)
    stay = lambda x: pltpu.with_memory_space_constraint(x, pltpu.HBM)
    size = 4 * depth * rows * lanes
    cost = lambda flops, moved: pl.CostEstimate(
        flops=flops * size, bytes_accessed=moved * size, transcendentals=0
    )
    wx, wy, spread = (keep(jnp.asarray(t)) for t in (wx, wy, spread))
    msg = pltpu.VMEM((8 * depth, lanes), f32)
    x_msg = pltpu.VMEM((4, 2, depth, lanes), f32)
    half = pltpu.VMEM((4 * depth, lanes), f32)

    def over_chips(column):
        return [
            (i * line + j, column(i, j)[0] * line + column(i, j)[1])
            for i in range(ring)
            for j in range(line)
        ]

    mate = lambda i, j: (i ^ 1, j)
    y_one = lambda i, j: (i, j ^ 1)
    y_two = lambda i, j: (i, (j + 1) % line if j % 2 else (j - 1) % line)
    first = lambda a, b: over_chips(lambda i, j: a(i, j) if i < 2 else b(i, j))
    both = ("gx", "gy")

    fields, chip, far_side, early_c, early_d = pl.pallas_call(
        edges_kernel,
        name="edge_sums",
        out_shape=(pltpu.VMEM((4,) + block, f32), x_msg, x_msg, msg, half),
        in_specs=[anywhere] * 4,
        out_specs=(vmem,) * 5,
        scratch_shapes=[pltpu.SemaphoreType.DMA((4 * pieces,))],
        compiler_params=params,
        cost_estimate=cost(20000, 12),
    )(*(stay(x) for x in (u, v, w, p)))
    early_c = lax.ppermute(early_c, both, first(y_one, mate))
    early_d = lax.ppermute(early_d, both, first(y_two, mate))

    far_side = pl.pallas_call(
        hold_kernel,
        name="hold",
        out_shape=x_msg,
        in_specs=[vmem],
        out_specs=vmem,
        input_output_aliases={0: 0},
        compiler_params=params,
        cost_estimate=cost(20000, 12),
    )(keep(far_side))
    got_far = lax.ppermute(
        far_side, "gx", [(i, (i + 1) % ring if i % 2 else (i - 1) % ring) for i in range(ring)]
    )

    parts = (jax.ShapeDtypeStruct((3,) + block, f32),) + (pltpu.VMEM(block, f32),) * 5
    scratch = [
        pltpu.VMEM(block, f32),
        pltpu.VMEM(block, f32),
        pltpu.SemaphoreType.DMA((2,)),
    ]
    lorentz, *part = pl.pallas_call(
        waiting_kernel,
        name="own_block_column_one",
        out_shape=parts,
        in_specs=[vmem] * 3 + [anywhere] * 2,
        out_specs=(anywhere,) + (vmem,) * 5,
        scratch_shapes=scratch,
        compiler_params=params,
        cost_estimate=cost(1, 1),
    )(keep(fields), wx, wy, keep(early_c), keep(early_d))

    late_c, late_d = pl.pallas_call(
        late_kernel,
        name="y_sums",
        out_shape=(msg, half),
        in_specs=[vmem, vmem, anywhere],
        out_specs=(vmem,) * 2,
        compiler_params=params,
        cost_estimate=cost(1, 1),
    )(*(keep(x) for x in (fields, chip, part[0])))
    late_c = lax.ppermute(late_c, both, first(mate, y_one))
    inner_two = lambda i, j: y_two(i, j) if 0 < j < line - 1 else mate(i, j)
    late_d = lax.ppermute(late_d, both, first(mate, inner_two))

    lorentz, *part = pl.pallas_call(
        rest_kernel,
        name="own_block",
        out_shape=parts,
        in_specs=[vmem] * 3 + [anywhere] + [vmem] * 5,
        out_specs=(anywhere,) + (vmem,) * 5,
        scratch_shapes=scratch,
        input_output_aliases={i + 3: i for i in range(6)},
        compiler_params=params,
        cost_estimate=cost(100, 12),
    )(keep(fields), wx, wy, lorentz, *(keep(x) for x in part))

    got_far = got_far.reshape(msg.shape)
    return pl.pallas_call(
        join_kernel,
        name="join",
        out_shape=(
            jax.ShapeDtypeStruct((3,) + block, f32),
            jax.ShapeDtypeStruct((3,) + block, f32),
            jax.ShapeDtypeStruct(block, f32),
        ),
        in_specs=[vmem] * 11 + [anywhere],
        out_specs=(anywhere,) * 3,
        scratch_shapes=[pltpu.VMEM(block, f32)] * 5
        + [pltpu.VMEM(msg.shape, f32), pltpu.VMEM(half.shape, f32), pltpu.VMEM(half.shape, f32)]
        + [pltpu.SemaphoreType.DMA((5,))],
        input_output_aliases={11: 0},
        compiler_params=params,
        cost_estimate=cost(10, 10),
    )(
        *(keep(x) for x in (got_far, early_c, early_d, late_c, late_d)),
        spread,
        *(keep(x) for x in part),
        lorentz,
    )


def solution(mesh):
    ring, line = mesh.shape["gx"], mesh.shape["gy"]
    cells = P(None, "gx", "gy")
    stacked = P(None, None, "gx", "gy")
    wx = x_operator(4096 // ring)
    wy = y_operators(512, line)
    spread = y_spread(512 // line, line)
    return jax.shard_map(
        functools.partial(local, wx, wy, spread, ring, line),
        mesh=mesh,
        in_specs=(cells,) * 4,
        out_specs=(stacked, stacked, cells),
        check_vma=False,
    )
```

```python
import functools
import math

import jax
import jax.numpy as jnp
import ml_dtypes
import numpy as np
from jax import lax
from jax.experimental import pallas as pl
from jax.experimental.pallas import tpu as pltpu
from jax.sharding import PartitionSpec as P

third = 1.0 / 3.0
near = 7.0 / 9.0
far = 1.0 / 36.0
bx = 0.6
by = 0.8

lam = (-3.0 + math.sqrt(5.0)) / 2.0
scale = 1.0 / (1.0 + 2.0 * third * lam)
log_lam = math.log(-lam)
gamma = scale * (near * (lam - 1.0 / lam) + far * (lam**2 - lam**-2))
edge = scale * (near * (lam**2 - 1.0) + far * (lam**3 - lam)) - gamma * lam

f32 = jnp.float32
bf16 = jnp.bfloat16
pieces = 1
own_step = 8
join_groups = (2, 2, 2, 2, 2, 2, 2, 2)


def halves(values):
    high = values.astype(bf16)
    return high, (values - high.astype(f32)).astype(bf16)


def host_halves(values):
    values = values.astype(np.float32)
    high = values.astype(ml_dtypes.bfloat16)
    low = (values - high.astype(np.float32)).astype(ml_dtypes.bfloat16)
    return high, low


def x_operator(count):
    h = lambda m: scale * lam ** np.abs(m)
    i = np.arange(count)
    m = i[:, None] - i[None, :]
    own = near * (h(m + 1) - h(m - 1)) + far * (h(m + 2) - h(m - 2))
    high, low = host_halves(own)
    return np.concatenate([high, low, high], axis=1)


def y_operators(total, blocks):
    a = np.eye(total)
    b = np.zeros((total, total))
    for j in range(2, total - 2):
        a[j, j - 1] = a[j, j + 1] = third
        b[j, j + 1], b[j, j - 1], b[j, j + 2], b[j, j - 2] = near, -near, far, -far
    a[0, 1] = a[-1, -2] = 2.0
    b[0, :3] = -2.5, 2.0, 0.5
    b[-1, -3:] = -0.5, -2.0, 2.5
    for j in (1, total - 2):
        a[j, j - 1] = a[j, j + 1] = 0.25
        b[j, j + 1], b[j, j - 1] = 0.75, -0.75
    whole = np.linalg.solve(a, b)
    size = total // blocks
    out = []
    for g in range(blocks):
        own = whole[g * size : (g + 1) * size, g * size : (g + 1) * size].T
        high, low = host_halves(own)
        out.append(np.block([[high, low], [high, np.zeros_like(low)]]))
    return np.stack(out)


def power(n):
    size = jnp.exp(n.astype(f32) * log_lam)
    return jnp.where((n & 1) == 0, size, -size)


def x_message(f, msg, planes, at_right):
    depth, rows, lanes = f.shape
    k = lax.broadcasted_iota(jnp.int32, (rows, lanes), 0)
    weights = jnp.where(at_right, gamma * power(rows - k), -gamma * power(k + 1))
    msg[0, planes] = jnp.sum(f * weights[None], axis=1)
    msg[1, planes] = jnp.where(at_right, edge * f[:, rows - 1, :], -edge * f[:, 0, :])


def y_messages(fields, msg_c, msg_d):
    _, depth, rows, lanes = fields.shape
    even_y = lax.rem(lax.axis_index("gy"), 2) == 0
    j = lax.broadcasted_iota(jnp.int32, (8, lanes), 1)
    row = lax.broadcasted_iota(jnp.int32, (8, lanes), 0)
    odd = (row & 1) == 1
    y_right = jnp.where(odd, jnp.where(j == lanes - 1, edge, 0.0), gamma * power(lanes - j))
    y_left = jnp.where(odd, jnp.where(j == 0, -edge, 0.0), -gamma * power(j + 1))
    high, low = halves(jnp.where((row < 2) == even_y, y_right, y_left))
    both = jnp.concatenate([high, low], axis=0)
    nt = (((1,), (1,)), ((), ()))
    for i in range(4):
        fh, fl = halves(fields[i].reshape(depth * rows, lanes))
        top = lax.dot_general(both, fh, nt, preferred_element_type=f32)
        rest = lax.dot_general(both, fl, nt, preferred_element_type=f32)
        sums = top[0:8] + top[8:16] + rest[0:8]
        for b in range(depth * rows // lanes):
            part = sums[:, b * lanes : (b + 1) * lanes]
            msg_c[pl.ds(8 * b + 2 * i, 2), :] = part[0:2]
            msg_d[pl.ds(8 * b + 2 * i, 2), :] = part[2:4]


def edges_kernel(u, v, w, p, fields, chip, far_side, early_c, early_d, sems):
    depth, rows, lanes = u.shape
    piece = depth // pieces
    copies = [
        [
            pltpu.make_async_copy(
                s.at[pl.ds(n * piece, piece)],
                fields.at[i, pl.ds(n * piece, piece)],
                sems.at[i * pieces + n],
            )
            for n in range(pieces)
        ]
        for i, s in enumerate((u, v, w, p))
    ]
    for field in copies:
        for c in field:
            c.start()
    gx = lax.axis_index("gx")
    even_x = lax.rem(gx, 2) == 0
    for i in range(4):
        for n in range(pieces):
            copies[i][n].wait()
            f = fields[i, pl.ds(n * piece, piece)]
            planes = pl.ds(n * piece, piece)
            x_message(f, chip.at[i], planes, even_x)
            x_message(f, far_side.at[i], planes, jnp.logical_not(even_x))

    @pl.when(gx < 2)
    def _():
        y_messages(fields, early_c, early_d)

    @pl.when(gx >= 2)
    def _():
        early_c[...] = chip[:2].reshape(early_c.shape)
        early_d[...] = chip[2:].reshape(early_d.shape)


def late_kernel(fields, chip, part, late_c, late_d):
    @pl.when(lax.axis_index("gx") < 2)
    def _():
        late_c[...] = chip[:2].reshape(late_c.shape)
        late_d[...] = chip[2:].reshape(late_d.shape)

    @pl.when(lax.axis_index("gx") >= 2)
    def _():
        y_messages(fields, late_c, late_d)


def own_block(fields, wx, wy_all, lorentz, lz_o, vx_o, vy_o, vz_o, dv_o, lx_s, ly_s, sems):
    _, depth, rows, lanes = fields.shape
    u, v, w, p = range(4)
    wy = wy_all.at[lax.axis_index("gy")]

    def dz(i, k):
        at = lambda s: fields[i, (k + s) & (depth - 1)]
        return (
            0.75 * (at(1) - at(-1)) - 0.15 * (at(2) - at(-2)) + (1.0 / 60.0) * (at(3) - at(-3))
        )


    @pl.loop(0, depth, step=own_step)
    def _(start):
        for n in range(own_step):
            k = start + n
            jz = by * fields[u, k] - bx * fields[v, k] - dz(p, k)
            lx_s[k] = -by * jz
            ly_s[k] = bx * jz

    put_x = pltpu.make_async_copy(lx_s, lorentz.at[0], sems.at[0])
    put_y = pltpu.make_async_copy(ly_s, lorentz.at[1], sems.at[1])
    put_x.start()
    put_y.start()
    def plane(k):
        split = [halves(fields[i, k]) for i in range(4)]
        highs = jnp.concatenate([s[0] for s in split], axis=0)
        lows = jnp.concatenate([s[1] for s in split], axis=0)
        y = jnp.dot(jnp.concatenate([highs, lows], axis=1), wy[...], preferred_element_type=f32)
        y = y[:, :lanes] + y[:, lanes:]
        wide_h = jnp.concatenate([s[0] for s in split], axis=1)
        wide_l = jnp.concatenate([s[1] for s in split], axis=1)
        x = jnp.dot(
            wx[...], jnp.concatenate([wide_h, wide_h, wide_l], axis=0), preferred_element_type=f32
        )
        yd = lambda i: y[i * rows : (i + 1) * rows]
        xd = lambda i: x[:, i * lanes : (i + 1) * lanes]
        lz_o[k] = bx * yd(p) - by * xd(p) - fields[w, k]
        vx_o[k] = yd(w) - dz(v, k)
        vy_o[k] = dz(u, k) - xd(w)
        vz_o[k] = xd(v) - yd(u)
        dv_o[k] = xd(u) + yd(v) + dz(w, k)

    @pl.loop(0, depth, step=own_step)
    def _(start):
        for n in range(own_step):
            plane(start + n)

    put_x.wait()
    put_y.wait()


def waiting_kernel(fields, wx, wy_all, early_c, early_d, *rest):
    @pl.when(lax.axis_index("gx") == 1)
    def _():
        own_block(fields, wx, wy_all, *rest)


def rest_kernel(fields, wx, wy_all, *rest):
    @pl.when(lax.axis_index("gx") != 1)
    def _():
        own_block(fields, wx, wy_all, *rest[6:])


def hold_kernel(message, held):
    pass


def y_spread(lanes, line):
    out = []
    j = np.arange(lanes)
    for g in range(line):
        table = np.zeros((16, 4, lanes))
        for side in range(2):
            from_left = (side == 1) == (g % 2 == 0)
            if (from_left and g == 0) or (not from_left and g == line - 1):
                continue
            away = j if from_left else lanes - 1 - j
            for field, (target, factor) in enumerate(((2, -1.0), (3, 1.0), (1, 1.0), (0, bx))):
                table[8 * side + 2 * field, target] = factor * lam**away
                table[8 * side + 2 * field + 1, target] = factor * (away == 0)
        table = table.reshape(16, 4 * lanes)
        table[np.abs(table) < 1e-37] = 0.0
        high, low = host_halves(table)
        out.append(np.concatenate([high, high, low], axis=0))
    return np.stack(out)


def join_kernel(
    got_far, early_c, early_d, late_c, late_d, spread_all, lz, vx, vy, vz, dv, lorentz_in,
    lorentz, vorticity, divergence, lz_s, vx_s, vy_s, vz_s, dv_s, chip_s, got_c, got_d, sems
):
    depth, rows, lanes = lz.shape
    gx = lax.axis_index("gx")
    even_x = lax.rem(gx, 2) == 0
    first = gx < 2
    spread = spread_all[lax.axis_index("gy")]
    got_c[...] = jnp.where(first, early_c[...], late_c[...])
    got_d[...] = jnp.where(first, early_d[...], late_d[...])
    middle = got_c.shape[0]
    chip_s[:middle] = jnp.where(first, late_c[...], early_c[...])
    chip_s[middle:] = jnp.where(first, late_d[...], early_d[...])
    i = lax.broadcasted_iota(jnp.int32, (rows, lanes), 0)
    fall_l, fall_r = power(i), power(rows - 1 - i)
    fall_chip = jnp.where(even_x, fall_r, fall_l)
    fall_far = jnp.where(even_x, fall_l, fall_r)
    sub = lax.broadcasted_iota(jnp.int32, (8, lanes), 0)
    low_far = jnp.where(jnp.logical_and(sub == 0, even_x), 1.0, 0.0)
    low_chip = jnp.where(jnp.logical_and(sub == 0, jnp.logical_not(even_x)), 1.0, 0.0)
    high_far = jnp.where(jnp.logical_and(sub == 7, jnp.logical_not(even_x)), 1.0, 0.0)
    high_chip = jnp.where(jnp.logical_and(sub == 7, even_x), 1.0, 0.0)

    def xc(f, k):
        at = lambda ref, kind: ref[pl.ds((2 * f + kind) * depth + k, 1), :]
        c = fall_far * at(got_far, 0) + fall_chip * at(chip_s, 0)
        far_e, chip_e = at(got_far, 1), at(chip_s, 1)
        head = c[:8] + low_far * far_e + low_chip * chip_e
        tail = c[rows - 8 :] + high_far * far_e + high_chip * chip_e
        return jnp.concatenate([head, c[8 : rows - 8], tail], axis=0)

    per = lanes // rows
    tn = (((0,), (0,)), ((), ()))
    targets = (
        (lz_s, lorentz.at[2]),
        (vx_s, vorticity.at[0]),
        (vy_s, vorticity.at[1]),
        (vz_s, vorticity.at[2]),
        (dv_s, divergence),
    )

    def puts(first_plane, last_plane):
        planes = pl.ds(first_plane, last_plane - first_plane)
        return [
            pltpu.make_async_copy(s.at[planes], d.at[planes], sems.at[n])
            for n, (s, d) in enumerate(targets)
        ]

    def group(first_plane, last_plane):
        for k in range(first_plane, last_plane):
            q = k % per
            if q == 0 or k == first_plane:
                rows_of = pl.ds(k // per * 8, 8)
                got = [m[rows_of, :] for m in (got_c, got_d)]
                high, low = halves(jnp.concatenate(got, axis=0))
                sums = jnp.concatenate([high, low, high], axis=0)
                yc = lax.dot_general(sums, spread, tn, preferred_element_type=f32)
            part = lambda t: yc[q * rows : (q + 1) * rows, t * lanes : (t + 1) * lanes]
            lz_s[k] = lz[k] + part(0) - by * xc(3, k)
            vx_s[k] = vx[k] + part(1)
            vy_s[k] = vy[k] - xc(2, k)
            vz_s[k] = vz[k] + part(2) + xc(1, k)
            dv_s[k] = dv[k] + part(3) + xc(0, k)
        for c in puts(first_plane, last_plane):
            c.start()

    start = 0
    for count in join_groups:
        pl.when(gx >= 0)(functools.partial(group, start, start + count))
        start += count
    for c in puts(0, depth):
        c.wait()


def local(wx, wy, spread, ring, line, u, v, w, p):
    depth, rows, lanes = u.shape
    block = (depth, rows, lanes)
    vmem = pl.BlockSpec(memory_space=pltpu.VMEM)
    anywhere = pl.BlockSpec(memory_space=pl.ANY)
    params = pltpu.CompilerParams(vmem_limit_bytes=24 * 2**20)
    keep = lambda x: pltpu.with_memory_space_constraint(x, pltpu.VMEM)
    stay = lambda x: pltpu.with_memory_space_constraint(x, pltpu.HBM)
    size = 4 * depth * rows * lanes
    cost = lambda flops, moved: pl.CostEstimate(
        flops=flops * size, bytes_accessed=moved * size, transcendentals=0
    )
    wx, wy, spread = (keep(jnp.asarray(t)) for t in (wx, wy, spread))
    msg = pltpu.VMEM((8 * depth, lanes), f32)
    x_msg = pltpu.VMEM((4, 2, depth, lanes), f32)
    half = pltpu.VMEM((4 * depth, lanes), f32)

    def over_chips(column):
        return [
            (i * line + j, column(i, j)[0] * line + column(i, j)[1])
            for i in range(ring)
            for j in range(line)
        ]

    mate = lambda i, j: (i ^ 1, j)
    y_one = lambda i, j: (i, j ^ 1)
    y_two = lambda i, j: (i, (j + 1) % line if j % 2 else (j - 1) % line)
    first = lambda a, b: over_chips(lambda i, j: a(i, j) if i < 2 else b(i, j))
    both = ("gx", "gy")

    fields, chip, far_side, early_c, early_d = pl.pallas_call(
        edges_kernel,
        name="edge_sums",
        out_shape=(pltpu.VMEM((4,) + block, f32), x_msg, x_msg, half, half),
        in_specs=[anywhere] * 4,
        out_specs=(vmem,) * 5,
        scratch_shapes=[pltpu.SemaphoreType.DMA((4 * pieces,))],
        compiler_params=params,
        cost_estimate=cost(20000, 12),
    )(*(stay(x) for x in (u, v, w, p)))
    early_c = lax.ppermute(early_c, both, first(y_one, mate))
    early_d = lax.ppermute(early_d, both, first(y_two, mate))

    far_side = pl.pallas_call(
        hold_kernel,
        name="hold",
        out_shape=x_msg,
        in_specs=[vmem],
        out_specs=vmem,
        input_output_aliases={0: 0},
        compiler_params=params,
        cost_estimate=cost(20000, 12),
    )(keep(far_side))
    got_far = lax.ppermute(
        far_side, "gx", [(i, (i + 1) % ring if i % 2 else (i - 1) % ring) for i in range(ring)]
    )

    parts = (jax.ShapeDtypeStruct((3,) + block, f32),) + (pltpu.VMEM(block, f32),) * 5
    scratch = [
        pltpu.VMEM(block, f32),
        pltpu.VMEM(block, f32),
        pltpu.SemaphoreType.DMA((2,)),
    ]
    lorentz, *part = pl.pallas_call(
        waiting_kernel,
        name="own_block_column_one",
        out_shape=parts,
        in_specs=[vmem] * 3 + [anywhere] * 2,
        out_specs=(anywhere,) + (vmem,) * 5,
        scratch_shapes=scratch,
        compiler_params=params,
        cost_estimate=cost(1, 1),
    )(keep(fields), wx, wy, keep(early_c), keep(early_d))

    late_c, late_d = pl.pallas_call(
        late_kernel,
        name="y_sums",
        out_shape=(half, half),
        in_specs=[vmem, vmem, anywhere],
        out_specs=(vmem,) * 2,
        compiler_params=params,
        cost_estimate=cost(1, 1),
    )(*(keep(x) for x in (fields, chip, part[0])))
    late_c = lax.ppermute(late_c, both, first(mate, y_one))
    inner_two = lambda i, j: y_two(i, j) if 0 < j < line - 1 else mate(i, j)
    late_d = lax.ppermute(late_d, both, first(mate, inner_two))

    lorentz, *part = pl.pallas_call(
        rest_kernel,
        name="own_block",
        out_shape=parts,
        in_specs=[vmem] * 3 + [anywhere] + [vmem] * 5,
        out_specs=(anywhere,) + (vmem,) * 5,
        scratch_shapes=scratch,
        input_output_aliases={i + 3: i for i in range(6)},
        compiler_params=params,
        cost_estimate=cost(100, 12),
    )(keep(fields), wx, wy, lorentz, *(keep(x) for x in part))

    got_far = got_far.reshape(msg.shape)
    return pl.pallas_call(
        join_kernel,
        name="join",
        out_shape=(
            jax.ShapeDtypeStruct((3,) + block, f32),
            jax.ShapeDtypeStruct((3,) + block, f32),
            jax.ShapeDtypeStruct(block, f32),
        ),
        in_specs=[vmem] * 11 + [anywhere],
        out_specs=(anywhere,) * 3,
        scratch_shapes=[pltpu.VMEM(block, f32)] * 5
        + [pltpu.VMEM(msg.shape, f32), pltpu.VMEM(half.shape, f32), pltpu.VMEM(half.shape, f32)]
        + [pltpu.SemaphoreType.DMA((5,))],
        input_output_aliases={11: 0},
        compiler_params=params,
        cost_estimate=cost(10, 10),
    )(
        *(keep(x) for x in (got_far, early_c, early_d, late_c, late_d)),
        spread,
        *(keep(x) for x in part),
        lorentz,
    )


def solution(mesh):
    ring, line = mesh.shape["gx"], mesh.shape["gy"]
    cells = P(None, "gx", "gy")
    stacked = P(None, None, "gx", "gy")
    wx = x_operator(4096 // ring)
    wy = y_operators(512, line)
    spread = y_spread(512 // line, line)
    return jax.shard_map(
        functools.partial(local, wx, wy, spread, ring, line),
        mesh=mesh,
        in_specs=(cells,) * 4,
        out_specs=(stacked, stacked, cells),
        check_vma=False,
    )
```
